32 devices in a mesh: groups: 2 (over x), hidden: 4 (over y, core), mp: 4 (over z).
Axes of the slice: x: 2, y: 2, z: 4, core: 2. Of those that a mesh axis runs over, the one named last changes fastest.
Arguments:
- tokens: bfloat16 [256, 8192], P(('groups', 'hidden'), 'mp'), parts along dimension 0, may hold values from -6 to 6
- up_codes: bfloat16 [8192, 24576], P('mp', 'hidden'), may hold values from -0.0625 to 0.0625
- up_scales: float32 [64, 192], P('mp', 'hidden'), may hold values from 0.5 to 2
- up_bias: bfloat16 [24576], P('hidden'), may hold values from -3 to 3
- down_codes: bfloat16 [24576, 8192], P('hidden', 'mp'), may hold values from -0.0390625 to 0.0390625
- down_scales: float32 [192, 64], P('hidden', 'mp'), may hold values from 0.5 to 2
- down_bias: bfloat16 [8192], P('mp'), may hold values from -3 to 3
- cotangent: bfloat16 [256, 8192], P(('groups', 'hidden'), 'mp'), parts along dimension 0, may hold values from -6 to 6
Outputs:
- ffn_output: bfloat16 [256, 8192], P(('groups', 'hidden'), 'mp'), parts along dimension 0
- grad_tokens: bfloat16 [256, 8192], P(('groups', 'hidden'), 'mp'), parts along dimension 0
- grad_up: bfloat16 [16384, 24576], P(('groups', 'mp'), 'hidden'), parts along dimension 0
- grad_down: bfloat16 [49152, 8192], P(('groups', 'hidden'), 'mp'), parts along dimension 0
- grad_up_bias: float32 [49152], P(('groups', 'hidden')), parts along dimension 0
The draws below stay inside these ranges and needn't reach their ends.
There are 2 independent parts, one for each index of `groups`. The reference program is written for one: setup_inputs(seed, part) draws one part's arguments, and reference() takes and returns one part's arrays. A program takes and returns all parts, laid end to end along the dimension named above; an argument that names none is the same for every part. Nothing has to cross between parts.
All inputs are finite; a program needn't handle non-finite values.
Results may differ from the reference program's by a relative error of at most 0.017.
Values may be sent and summed in bfloat16 or wider, within the bound.
No kernel may reach another device: no remote copies, remote signals or barrier semaphores. Data moves between devices by JAX's collectives and lax.ppermute only.
A program may use at most 384 MiB of HBM per device.

```python
import math
import jax
import jax.numpy as jnp
from jax import lax

D = 8192
FF = 24576
QB = 128
TOKENS = 128
N_MP = 4


def level_of(stream_key, shape, split, least, top_value):
    def one(dim, parts):
        steps = jax.random.uniform(jax.random.fold_in(jax.random.fold_in(stream_key, 6), dim), (parts,), jnp.float32, least / len(split), top_value / len(split))
        return jnp.repeat(jnp.exp(steps), shape[dim] // parts).reshape((-1,) + (1,) * (len(shape) - dim - 1))

    factor_of = one(*split[0])
    for cut in split[1:]:
        factor_of = factor_of * one(*cut)
    return factor_of


def gaussian(key, shape, deviation, most, pieces=(), held_as=jnp.bfloat16):
    loudness = level_of(key, shape, pieces, -0.22, 0.18) if pieces else 1.0
    result = jax.random.normal(key, shape, jnp.float32) * deviation * loudness
    return jnp.minimum(jnp.maximum(result, -most), most).astype(held_as)


def setup_inputs(seed: int = 0, part: int = 0) -> dict:
    key_list = jax.random.split(jax.random.key(seed), 9)
    part_splits = jax.random.split(jax.random.fold_in(key_list[8], part), 9)
    tokens = gaussian(part_splits[0], (TOKENS, D), 1.0, 6.0, ((0, 4), (1, 4)))
    up_codes = gaussian(key_list[1], (D, FF), D ** -0.5, 0.0625, ((0, 4), (1, 4)))
    up_scales = jnp.clip(jnp.exp(math.log(2.0) - 1.3862944 * jax.random.uniform(key_list[2], (D // QB, FF // QB), jnp.float32) ** level_of(key_list[2], (D // QB, FF // QB), ((0, 4), (1, 4)), -0.2, 0.2)), 0.5, 2.0)
    up_bias = gaussian(key_list[3], (FF,), 0.5, 3.0, ((0, 4),))
    down_codes = gaussian(key_list[4], (FF, D), FF ** -0.5, 0.0390625, ((0, 4), (1, 4)))
    down_scales = jnp.clip(jnp.exp(math.log(2.0) - 1.3862944 * jax.random.uniform(key_list[5], (FF // QB, D // QB), jnp.float32) ** level_of(key_list[5], (FF // QB, D // QB), ((0, 4), (1, 4)), -0.2, 0.2)), 0.5, 2.0)
    down_bias = gaussian(key_list[6], (D,), 0.5, 3.0, ((0, 4),))
    cotangent = gaussian(part_splits[7], (TOKENS, D), 1.0, 6.0, ((0, 4), (1, 4)))
    return {"tokens": tokens, "up_codes": up_codes, "up_scales": up_scales, "up_bias": up_bias, "down_codes": down_codes, "down_scales": down_scales, "down_bias": down_bias, "cotangent": cotangent}


root_two_pi = 0.7978845608028654
cubic_coef = 0.044715


def gelu_value(argument):
    inner_arg = root_two_pi * (argument + cubic_coef * argument * argument * argument)
    return 0.5 * argument * (1.0 + jnp.tanh(inner_arg))


def gelu_slope(argument):
    inner_arg = root_two_pi * (argument + cubic_coef * argument * argument * argument)
    tangent = jnp.tanh(inner_arg)
    return 0.5 * (1.0 + tangent) + 0.5 * argument * (1.0 - tangent * tangent) * root_two_pi * (1.0 + 3.0 * cubic_coef * argument * argument)


def dequantize(weight_codes, block_scales):
    row_count, col_count = weight_codes.shape
    scale_rows, scale_cols = block_scales.shape
    blocks = weight_codes.astype(jnp.float32).reshape(scale_rows, row_count // scale_rows, scale_cols, col_count // scale_cols)
    scaled = blocks * block_scales.astype(jnp.float32)[:, None, :, None]
    return scaled.reshape(row_count, col_count).astype(jnp.bfloat16)


def product(left_side, right_side):
    return jnp.dot(left_side.astype(jnp.float32), right_side.astype(jnp.float32), precision=lax.Precision.HIGHEST)


def rounded(partial_sum):
    narrow = lax.optimization_barrier(partial_sum.astype(jnp.bfloat16))
    return narrow.astype(jnp.float32)


def reference(tokens, up_codes, up_scales, up_bias, down_codes, down_scales, down_bias, cotangent):
    w_up = dequantize(up_codes, up_scales)
    w_down = dequantize(down_codes, down_scales)
    slab_width = D // N_MP
    preact = jnp.zeros((TOKENS, FF), jnp.float32)
    grad_act = jnp.zeros((TOKENS, FF), jnp.float32)
    for slab in range(N_MP):
        lower = slab * slab_width
        upper = lower + slab_width
        preact = preact + rounded(product(tokens[:, lower:upper], w_up[lower:upper, :]))
        grad_act = grad_act + rounded(product(cotangent[:, lower:upper], w_down[:, lower:upper].T))
    preact = preact + up_bias.astype(jnp.float32)
    activation = gelu_value(preact).astype(jnp.bfloat16)
    ffn_output = (product(activation, w_down) + down_bias.astype(jnp.float32)).astype(jnp.bfloat16)
    grad_preact = (grad_act * gelu_slope(preact)).astype(jnp.bfloat16)
    grad_up_bias = jnp.sum(grad_preact.astype(jnp.float32), axis=0)
    grad_down = product(activation.T, cotangent).astype(jnp.bfloat16)
    grad_up = product(tokens.T, grad_preact).astype(jnp.bfloat16)
    grad_tokens = product(grad_preact, w_up.T).astype(jnp.bfloat16)
    return (ffn_output, grad_tokens, grad_up, grad_down, grad_up_bias)
```

```python
import functools

import jax
import jax.numpy as jnp
from jax import lax
from jax.experimental import pallas as pl
from jax.experimental.pallas import tpu as pltpu
from jax.sharding import PartitionSpec as P

root_two_pi = 0.7978845608028654
cubic_coef = 0.044715
LANES = 128
VMEM_LIMIT = 40 * 1024 * 1024


def gelu_value(argument):
    inner_arg = root_two_pi * (argument + cubic_coef * argument * argument * argument)
    return 0.5 * argument * (1.0 + jnp.tanh(inner_arg))


def gelu_slope(argument):
    inner_arg = root_two_pi * (argument + cubic_coef * argument * argument * argument)
    tangent = jnp.tanh(inner_arg)
    return 0.5 * (1.0 + tangent) + 0.5 * argument * (1.0 - tangent * tangent) * root_two_pi * (
        1.0 + 3.0 * cubic_coef * argument * argument
    )


def dequantize(weight_codes, block_scales):
    row_count, col_count = weight_codes.shape
    scale_rows, scale_cols = block_scales.shape
    blocks = weight_codes.astype(jnp.float32).reshape(
        scale_rows, row_count // scale_rows, scale_cols, col_count // scale_cols
    )
    scaled = blocks * block_scales[:, None, :, None]
    return scaled.reshape(row_count, col_count).astype(jnp.bfloat16)


def plain_product(left_side, right_side):
    return jnp.dot(left_side, right_side, preferred_element_type=jnp.float32)


def product_transposed(left_side, right_side):
    return lax.dot_general(
        left_side, right_side, (((1,), (1,)), ((), ())), preferred_element_type=jnp.float32
    )


def transposed_product(left_side, right_side):
    return lax.dot_general(
        left_side, right_side, (((0,), (0,)), ((), ())), preferred_element_type=jnp.float32
    )


def up_kernel(side, block_ref, tokens_ref, codes_ref, scales_ref, out_ref, weights):
    for row in range(codes_ref.shape[0] // side):
        rows = slice(row * side, (row + 1) * side)
        weights[rows, :] = (
            codes_ref[rows, :].astype(jnp.float32) * scales_ref[row : row + 1, :]
        ).astype(jnp.bfloat16)
    out_ref[...] = plain_product(tokens_ref[...], weights[...]).astype(out_ref.dtype)


def down_scaled(side, first_row, codes_ref, scales_ref, weights):
    for row in range(codes_ref.shape[0] // side):
        rows = slice(row * side, (row + 1) * side)
        weights[rows, :] = (
            codes_ref[rows, :].astype(jnp.float32) * scales_ref[pl.ds(first_row + row, 1), :]
        ).astype(jnp.bfloat16)


def down_kernel(side, tiles, block_ref, cot_ref, codes_ref, scales_ref, out_ref, weights):
    per_tile = codes_ref.shape[0] // side
    first_row = (block_ref[0] * tiles + pl.program_id(0)) * per_tile
    down_scaled(side, first_row, codes_ref, scales_ref, weights)
    out_ref[...] = product_transposed(cot_ref[...], weights[...]).astype(out_ref.dtype)


def output_kernel(side, tiles, fresh, block_ref, act_ref, codes_ref, scales_ref, cot_ref, *refs):
    out_ref, grad_ref, weights = refs[-3:]
    per_tile = codes_ref.shape[0] // side
    first_row = (block_ref[0] * tiles + pl.program_id(0)) * per_tile

    @pl.when(pl.program_id(0) == 0)
    def _():
        out_ref[...] = jnp.zeros_like(out_ref) if fresh else refs[0][...]

    down_scaled(side, first_row, codes_ref, scales_ref, weights)
    out_ref[...] += plain_product(act_ref[...], weights[...])
    grad_ref[...] = transposed_product(act_ref[...], cot_ref[...]).astype(grad_ref.dtype)


def input_kernel(side, fresh, block_ref, pre_ref, codes_ref, scales_ref, turned_ref, *refs):
    out_ref, grad_ref, bias_ref, weights = refs[-4:]

    @pl.when(pl.program_id(0) == 0)
    def _():
        out_ref[...] = jnp.zeros_like(out_ref) if fresh else refs[0][...]

    for row in range(codes_ref.shape[0] // side):
        rows = slice(row * side, (row + 1) * side)
        weights[rows, :] = (
            codes_ref[rows, :].astype(jnp.float32) * scales_ref[row : row + 1, :]
        ).astype(jnp.bfloat16)
    out_ref[...] += product_transposed(pre_ref[...], weights[...])
    grad_ref[...] = plain_product(turned_ref[...], pre_ref[...]).astype(grad_ref.dtype)
    bias_ref[...] = jnp.sum(pre_ref[...].astype(jnp.float32), axis=0, keepdims=True)


def cost_of(token_count, width, hidden_count, products, passes):
    return pl.CostEstimate(
        flops=2 * products * token_count * width * hidden_count,
        bytes_accessed=2 * passes * width * hidden_count,
        transcendentals=0,
    )


def whole_spec(shape):
    return pl.BlockSpec(shape, lambda step, block: (0,) * len(shape))


def call(kernel, tiles, in_specs, out_specs, out_shape, scratch, cost, aliases=None):
    return pl.pallas_call(
        kernel,
        grid_spec=pltpu.PrefetchScalarGridSpec(
            num_scalar_prefetch=1,
            grid=(tiles,),
            in_specs=in_specs,
            out_specs=out_specs,
            scratch_shapes=scratch,
        ),
        out_shape=out_shape,
        input_output_aliases=aliases or {},
        cost_estimate=cost,
        compiler_params=pltpu.CompilerParams(vmem_limit_bytes=VMEM_LIMIT),
    )


def tile_of(block_width):
    return next(width for width in (512, 256, 128) if block_width % width == 0)


def ring_program(mp_count, hidden_count):
    ring = [(i, (i + 1) % mp_count) for i in range(mp_count)]
    bits = [1 << bit for bit in reversed(range(hidden_count.bit_length() - 1))]

    def partner_pairs(bit):
        return [(i, i ^ bit) for i in range(hidden_count)]

    def gathered_rows(own_rows):
        held = own_rows
        for bit in bits:
            held = jnp.concatenate([held, lax.ppermute(held, "hidden", partner_pairs(bit))])
        return held

    def scattered_sum(partial_sum):
        held = partial_sum
        for bit in reversed(bits):
            half = held.shape[0] // 2
            sent = held[half:].astype(jnp.bfloat16)
            held = held[:half] + lax.ppermute(sent, "hidden", partner_pairs(bit)).astype(
                jnp.float32
            )
        return held

    def on_device(
        tokens, up_codes, up_scales, up_bias, down_codes, down_scales, down_bias, cotangent
    ):
        width, hidden = up_codes.shape
        side = width // up_scales.shape[0]
        rows = tokens.shape[0] * hidden_count
        block_width = hidden // mp_count
        tile = tile_of(block_width)
        tiles = block_width // tile
        me = lax.axis_index("mp").astype(jnp.int32)

        token_rows = gathered_rows(tokens)
        cot_rows = gathered_rows(cotangent)
        up_wide = jnp.repeat(up_scales, side, axis=1)
        down_wide = jnp.repeat(down_scales, side, axis=1)
        turned_tokens = token_rows.T

        def block_number(back):
            return ((me + 2 * mp_count - back) % mp_count).reshape(1)

        up_codes_spec = pl.BlockSpec(
            (width, tile), lambda step, block: (0, block[0] * tiles + step)
        )
        up_scales_spec = pl.BlockSpec(
            (up_wide.shape[0], tile), lambda step, block: (0, block[0] * tiles + step)
        )
        down_codes_spec = pl.BlockSpec(
            (tile, width), lambda step, block: (block[0] * tiles + step, 0)
        )
        share_spec = pl.BlockSpec((rows, tile), lambda step, block: (0, step))
        share_shape = jax.ShapeDtypeStruct((rows, block_width), jnp.bfloat16)

        def up_share(back):
            return call(
                functools.partial(up_kernel, side),
                tiles,
                [whole_spec((rows, width)), up_codes_spec, up_scales_spec],
                share_spec,
                share_shape,
                [pltpu.VMEM((width, tile), jnp.bfloat16)],
                cost_of(rows, width, block_width, 1, 1),
            )(block_number(back), token_rows, up_codes, up_wide)

        def down_share(back):
            return call(
                functools.partial(down_kernel, side, tiles),
                tiles,
                [whole_spec((rows, width)), down_codes_spec, whole_spec(down_wide.shape)],
                share_spec,
                share_shape,
                [pltpu.VMEM((tile, width), jnp.bfloat16)],
                cost_of(rows, width, block_width, 1, 1),
            )(block_number(back), cot_rows, down_codes, down_wide)

        def output_step(back, act_block, held):
            fresh = held is None
            carried = [] if fresh else list(held)
            carried_specs = (
                [] if fresh else [whole_spec((rows, width)), pl.BlockSpec(memory_space=pl.ANY)]
            )
            return call(
                functools.partial(output_kernel, side, tiles, fresh),
                tiles,
                [share_spec, down_codes_spec, whole_spec(down_wide.shape), whole_spec((rows, width))]
                + carried_specs,
                [whole_spec((rows, width)), down_codes_spec],
                [
                    jax.ShapeDtypeStruct((rows, width), jnp.float32),
                    jax.ShapeDtypeStruct((hidden, width), jnp.bfloat16),
                ],
                [pltpu.VMEM((tile, width), jnp.bfloat16)],
                cost_of(rows, width, block_width, 2, 2),
                {} if fresh else {6: 1},
            )(block_number(back), act_block, down_codes, down_wide, cot_rows, *carried)

        def input_step(back, pre_block, held):
            fresh = held is None
            carried = [] if fresh else list(held)
            carried_specs = (
                []
                if fresh
                else [
                    whole_spec((rows, width)),
                    pl.BlockSpec(memory_space=pl.ANY),
                    pl.BlockSpec(memory_space=pl.ANY),
                ]
            )
            bias_spec = pl.BlockSpec((1, tile), lambda step, block: (0, block[0] * tiles + step))
            return call(
                functools.partial(input_kernel, side, fresh),
                tiles,
                [share_spec, up_codes_spec, up_scales_spec, whole_spec((width, rows))]
                + carried_specs,
                [whole_spec((rows, width)), up_codes_spec, bias_spec],
                [
                    jax.ShapeDtypeStruct((rows, width), jnp.float32),
                    jax.ShapeDtypeStruct((width, hidden), jnp.bfloat16),
                    jax.ShapeDtypeStruct((1, hidden), jnp.float32),
                ],
                [pltpu.VMEM((width, tile), jnp.bfloat16)],
                cost_of(rows, width, block_width, 2, 2),
                {} if fresh else {6: 1, 7: 2},
            )(block_number(back), pre_block, up_codes, up_wide, turned_tokens, *carried)

        def passed_on(block):
            return lax.ppermute(block, "mp", ring)

        def added(left, right):
            return left.astype(jnp.float32) + right.astype(jnp.float32)

        up_sum = down_sum = None
        for step in range(mp_count - 1):
            up_part = up_share(step + 1)
            up_sum = passed_on(
                up_part if up_sum is None else added(up_sum, up_part).astype(jnp.bfloat16)
            )
            down_part = down_share(step + 1)
            down_sum = passed_on(
                down_part if down_sum is None else added(down_sum, down_part).astype(jnp.bfloat16)
            )
        own_bias = lax.dynamic_slice(up_bias, (me * block_width,), (block_width,))
        preact = added(up_sum, up_share(0)) + own_bias.astype(jnp.float32)
        act_block = gelu_value(preact).astype(jnp.bfloat16)
        grad_act = added(down_sum, down_share(0))
        pre_block = (grad_act * gelu_slope(preact)).astype(jnp.bfloat16)

        output_held = input_held = None
        for back in range(mp_count):
            next_act = passed_on(act_block) if back < mp_count - 1 else None
            output_held = output_step(back, act_block, output_held)
            next_pre = passed_on(pre_block) if back < mp_count - 1 else None
            input_held = input_step(back, pre_block, input_held)
            act_block, pre_block = next_act, next_pre
        output_partial, grad_down = output_held
        tokens_partial, grad_up, grad_up_bias = input_held
        ffn_output = (scattered_sum(output_partial) + down_bias.astype(jnp.float32)).astype(
            jnp.bfloat16
        )
        grad_tokens = scattered_sum(tokens_partial).astype(jnp.bfloat16)
        return (ffn_output, grad_tokens, grad_up, grad_down, grad_up_bias.reshape(hidden))

    return on_device


def plain_program(
    tokens, up_codes, up_scales, up_bias, down_codes, down_scales, down_bias, cotangent
):
    w_up = dequantize(up_codes, up_scales)
    w_down = dequantize(down_codes, down_scales)
    cot_rows = lax.all_gather(cotangent, "hidden", axis=0, tiled=True)
    token_rows = lax.all_gather(tokens, "hidden", axis=0, tiled=True)
    bias_up = up_bias.astype(jnp.float32)

    def summed(share, axis):
        return lax.psum_scatter(
            share.astype(jnp.bfloat16), axis, scatter_dimension=0, tiled=True
        ).astype(jnp.float32)

    preact_share = summed(plain_product(token_rows, w_up), "mp") + bias_up
    act_share = gelu_value(preact_share).astype(jnp.bfloat16)
    act_rows = lax.all_gather(act_share, "mp", axis=0, tiled=True)
    grad_share = summed(product_transposed(cot_rows, w_down), "mp")
    grad_pre_share = (grad_share * gelu_slope(preact_share)).astype(jnp.bfloat16)
    grad_pre_rows = lax.all_gather(grad_pre_share, "mp", axis=0, tiled=True)
    output_sum = summed(plain_product(act_rows, w_down), "hidden")
    ffn_output = (output_sum + down_bias.astype(jnp.float32)).astype(jnp.bfloat16)
    grad_tokens = summed(product_transposed(grad_pre_rows, w_up), "hidden").astype(jnp.bfloat16)
    grad_up_bias = jnp.sum(grad_pre_rows, axis=0, dtype=jnp.float32)
    grad_down = transposed_product(act_rows, cot_rows).astype(jnp.bfloat16)
    grad_up = transposed_product(token_rows, grad_pre_rows).astype(jnp.bfloat16)
    return (ffn_output, grad_tokens, grad_up, grad_down, grad_up_bias)


def solution(mesh):
    mp_count, hidden_count = mesh.shape["mp"], mesh.shape["hidden"]

    def on_device(*arrays):
        hidden = arrays[1].shape[1]
        whole_blocks = hidden % (mp_count * LANES) == 0
        if whole_blocks and mp_count > 1 and hidden_count & (hidden_count - 1) == 0:
            return ring_program(mp_count, hidden_count)(*arrays)
        return plain_program(*arrays)

    in_specs = (
        P(("groups", "hidden"), "mp"),
        P("mp", "hidden"),
        P("mp", "hidden"),
        P("hidden"),
        P("hidden", "mp"),
        P("hidden", "mp"),
        P("mp"),
        P(("groups", "hidden"), "mp"),
    )
    out_specs = (
        P(("groups", "hidden"), "mp"),
        P(("groups", "hidden"), "mp"),
        P(("groups", "mp"), "hidden"),
        P(("groups", "hidden"), "mp"),
        P(("groups", "hidden")),
    )
    return jax.shard_map(
        on_device, mesh=mesh, in_specs=in_specs, out_specs=out_specs, check_vma=False
    )
```

```python
import functools

import jax
import jax.numpy as jnp
from jax import lax
from jax.experimental import pallas as pl
from jax.experimental.pallas import tpu as pltpu
from jax.sharding import PartitionSpec as P

root_two_pi = 0.7978845608028654
cubic_coef = 0.044715
LANES = 128
MIB = 1024 * 1024
COST_SCALE = 3
SHARE_MIB = 4
GRADIENT_MIB = 12
KEEP_UP = (0, 3)
KEEP_DOWN = (0, 3)


def gelu_value(argument):
    inner_arg = root_two_pi * (argument + cubic_coef * argument * argument * argument)
    return 0.5 * argument * (1.0 + jnp.tanh(inner_arg))


def gelu_slope(argument):
    inner_arg = root_two_pi * (argument + cubic_coef * argument * argument * argument)
    tangent = jnp.tanh(inner_arg)
    return 0.5 * (1.0 + tangent) + 0.5 * argument * (1.0 - tangent * tangent) * root_two_pi * (
        1.0 + 3.0 * cubic_coef * argument * argument
    )


def dequantize(weight_codes, block_scales):
    row_count, col_count = weight_codes.shape
    scale_rows, scale_cols = block_scales.shape
    blocks = weight_codes.astype(jnp.float32).reshape(
        scale_rows, row_count // scale_rows, scale_cols, col_count // scale_cols
    )
    scaled = blocks * block_scales[:, None, :, None]
    return scaled.reshape(row_count, col_count).astype(jnp.bfloat16)


def plain_product(left_side, right_side):
    return jnp.dot(left_side, right_side, preferred_element_type=jnp.float32)


def product_transposed(left_side, right_side):
    return lax.dot_general(
        left_side, right_side, (((1,), (1,)), ((), ())), preferred_element_type=jnp.float32
    )


def transposed_product(left_side, right_side):
    return lax.dot_general(
        left_side, right_side, (((0,), (0,)), ((), ())), preferred_element_type=jnp.float32
    )


def up_scaled(side, weights_ref, scales_ref, block, first, count):
    columns = slice(first, first + count)
    width = weights_ref.shape[1]
    scale_columns = pl.ds(pl.multiple_of(block * width + first, LANES), count)
    for row in range(weights_ref.shape[0] // side):
        rows = slice(row * side, (row + 1) * side)
        weights_ref[rows, columns] = (
            weights_ref[rows, columns].astype(jnp.float32) * scales_ref[row : row + 1, scale_columns]
        ).astype(jnp.bfloat16)
    return weights_ref[:, columns]


def down_scaled(side, weights_ref, scales_ref, block, first, count):
    for row in range(first // side, (first + count) // side):
        rows = slice(row * side, (row + 1) * side)
        weights_ref[rows, :] = (
            weights_ref[rows, :].astype(jnp.float32) * scales_ref[block, row : row + 1, :]
        ).astype(jnp.bfloat16)
    return weights_ref[first : first + count, :]


def code_copies(up, piece, codes_ref, weights_ref, sems, block):
    block_width = weights_ref.shape[1 if up else 0]
    copies = []
    for index in range(block_width // piece):
        there = pl.ds(pl.multiple_of(block * block_width + index * piece, LANES), piece)
        here = slice(index * piece, (index + 1) * piece)
        copies.append(
            pltpu.make_async_copy(
                codes_ref.at[:, there] if up else codes_ref.at[there, :],
                weights_ref.at[:, here] if up else weights_ref.at[here, :],
                sems.at[index],
            )
        )
    return copies


def share_kernel(side, up, piece, part_count, sum_in, turn, block_ref, *refs):
    refs = list(refs)
    block = block_ref[0]
    parts = [refs.pop(0) for _ in range(part_count)]
    rows_ref = None if part_count else refs.pop(0)
    codes_ref, scales_ref = refs.pop(0), refs.pop(0)
    sum_ref = refs.pop(0) if sum_in else None
    out_ref = refs.pop(0)
    if part_count:
        rows_ref = refs.pop(0)
    turned_ref = refs.pop(0) if turn else None
    weights_ref, sems = refs
    copies = code_copies(up, piece, codes_ref, weights_ref, sems, block)
    own_copy = None
    if part_count:
        depth = parts[0].shape[0]
        own_copy = pltpu.make_async_copy(parts[0], rows_ref.at[:depth, :], sems.at[len(copies)])
        own_copy.start()
    for copy in copies:
        copy.start()
    if part_count:
        for index, part in enumerate(parts):
            if index == 0:
                continue
            rows_ref[index * depth : (index + 1) * depth, :] = part[...]
        own_copy.wait()
    if turn:
        turned_ref[...] = rows_ref[...].T
    for index, copy in enumerate(copies):
        copy.wait()
        columns = slice(index * piece, (index + 1) * piece)
        if up:
            weights = up_scaled(side, weights_ref, scales_ref, block, index * piece, piece)
            share = plain_product(rows_ref[...], weights)
        else:
            weights = down_scaled(side, weights_ref, scales_ref, block, index * piece, piece)
            share = product_transposed(rows_ref[...], weights)
        if sum_in:
            share = share.astype(jnp.bfloat16).astype(jnp.float32) + sum_ref[:, columns].astype(
                jnp.float32
            )
        out_ref[:, columns] = share.astype(jnp.bfloat16)


def activation_kernel(sum_ref, share_ref, bias_ref, act_ref, slope_ref):
    preact = (
        sum_ref[...].astype(jnp.float32)
        + share_ref[...].astype(jnp.float32)
        + bias_ref[...].astype(jnp.float32)
    )
    act_ref[...] = gelu_value(preact).astype(jnp.bfloat16)
    slope_ref[...] = gelu_slope(preact)


def product_kernel(act_ref, weights_ref, total_in, after_ref, kept_ref, sent_ref):
    total = (total_in[...] + product_transposed(weights_ref[...], act_ref[...])).T
    half = total.shape[0] // 2
    kept_ref[...] = total[:half, :]
    sent_ref[...] = total[half:, :].astype(jnp.bfloat16)


def gradient_kernel(side, up, piece, fresh, last, kept_weights, summed, block_ref, *refs):
    refs = list(refs)
    block = block_ref[0]
    block_act, rows_ref = refs.pop(0), refs.pop(0)
    weights_ref = refs.pop(0) if kept_weights and summed else None
    codes_ref, scales_ref = (None, None) if kept_weights else (refs.pop(0), refs.pop(0))
    if not fresh:
        total_in = refs.pop(0) if summed else None
        refs.pop(0)
        bias_in = refs.pop(0) if up else None
    refs.pop(0)
    if last and summed:
        kept_ref, sent_ref = refs.pop(0), refs.pop(0)
    elif summed:
        total_ref = refs.pop(0)
    grad_ref = refs.pop(0)
    bias_ref = refs.pop(0) if up else None
    if last and summed:
        total_ref = refs.pop(0)
    staged, out_sems = refs.pop(0), refs.pop(0)
    copies = [None] * (block_act.shape[1] // piece)
    if not kept_weights:
        weights_ref, sems = refs
        copies = code_copies(up, piece, codes_ref, weights_ref, sems, block)
        for copy in copies:
            copy.start()
    if up and not fresh:
        bias_ref[...] = bias_in[...]
    block_width, slots = block_act.shape[1], staged.shape[0]
    writes = []
    for index, copy in enumerate(copies):
        columns = slice(index * piece, (index + 1) * piece)
        there = pl.ds(pl.multiple_of(block * block_width + index * piece, LANES), piece)
        write = pltpu.make_async_copy(
            staged.at[index % slots],
            grad_ref.at[:, there] if up else grad_ref.at[there, :],
            out_sems.at[index % slots],
        )
        if index >= slots:
            writes[index - slots].wait()
        act = block_act[:, columns]
        if up:
            gradient = plain_product(rows_ref[...], act)
            bias_ref[0:1, there] = jnp.sum(act.astype(jnp.float32), axis=0, keepdims=True)
        else:
            gradient = transposed_product(act, rows_ref[...])
        staged[index % slots] = gradient.astype(jnp.bfloat16)
        write.start()
        writes.append(write)
        if not summed:
            continue
        if copy is not None:
            copy.wait()
            scaled = up_scaled if up else down_scaled
            scaled(side, weights_ref, scales_ref, block, index * piece, piece)
        if up:
            share = product_transposed(weights_ref[:, columns], act)
        else:
            share = plain_product(act, weights_ref[columns, :])
        if index == 0 and fresh:
            total_ref[...] = share
        elif index == 0:
            total_ref[...] = total_in[...] + share
        else:
            total_ref[...] += share
    if last and summed:
        half = total_ref.shape[0] // 2
        kept_ref[...] = total_ref[:half, :]
        sent_ref[...] = total_ref[half:, :].astype(jnp.bfloat16)
    for write in writes[-slots:]:
        write.wait()


def cost_of(token_count, width, hidden_count, products, passes):
    return pl.CostEstimate(
        flops=COST_SCALE * 2 * products * token_count * width * hidden_count,
        bytes_accessed=COST_SCALE * 2 * passes * width * hidden_count,
        transcendentals=0,
    )


ANY_SPEC = pl.BlockSpec(memory_space=pl.ANY)
VMEM_SPEC = pl.BlockSpec(memory_space=pltpu.VMEM)
SMEM_SPEC = pl.BlockSpec(memory_space=pltpu.SMEM)


class Operands:
    def __init__(self, block):
        self.arrays, self.specs = [block], [SMEM_SPEC]

    def add(self, array, spec=VMEM_SPEC):
        self.arrays.append(array)
        self.specs.append(spec)


def call(name, kernel, operands, outs, scratch, cost, limit, aliases=None):
    return pl.pallas_call(
        kernel,
        in_specs=operands.specs,
        out_specs=[spec for _, spec in outs],
        scratch_shapes=scratch,
        out_shape=[shape for shape, _ in outs],
        input_output_aliases=aliases or {},
        cost_estimate=cost,
        name=name,
        compiler_params=pltpu.CompilerParams(vmem_limit_bytes=limit * MIB),
    )(*operands.arrays)


class Sizes:
    def __init__(self, rows, width, hidden, block_width, side):
        self.rows, self.width, self.hidden = rows, width, hidden
        self.block_width, self.side = block_width, side

    def piece(self, most):
        return next(
            size for size in (512, 256, 128) if size <= most and self.block_width % size == 0
        )

    def weights_shape(self, up):
        return (self.width, self.block_width) if up else (self.block_width, self.width)


def share_call(sizes, up, block, rows, codes, scales, sum_in, keep, turn=False):
    parts = rows if isinstance(rows, list) else []
    operands = Operands(block)
    for index, part in enumerate(parts or [rows]):
        operands.add(part, ANY_SPEC if parts and index == 0 else VMEM_SPEC)
    operands.add(pltpu.with_memory_space_constraint(codes, pltpu.HBM), ANY_SPEC)
    operands.add(scales)
    if sum_in is not None:
        operands.add(pltpu.with_memory_space_constraint(sum_in, pltpu.VMEM))
    outs = [(pltpu.VMEM((sizes.rows, sizes.block_width), jnp.bfloat16), VMEM_SPEC)]
    if parts:
        outs.append((jax.ShapeDtypeStruct((sizes.rows, sizes.width), jnp.bfloat16), VMEM_SPEC))
    if turn:
        outs.append((jax.ShapeDtypeStruct((sizes.width, sizes.rows), jnp.bfloat16), VMEM_SPEC))
    weights = pltpu.VMEM(sizes.weights_shape(up), jnp.bfloat16)
    if keep:
        outs.append((weights, VMEM_SPEC))
    piece = sizes.piece(256 if up else 512)
    return call(
        "up_share" if up else "down_share",
        functools.partial(share_kernel, sizes.side, up, piece, len(parts), sum_in is not None, turn),
        operands,
        outs,
        ([] if keep else [weights])
        + [pltpu.SemaphoreType.DMA((sizes.block_width // piece + 1,))],
        cost_of(sizes.rows, sizes.width, sizes.block_width, 1, 1),
        SHARE_MIB if keep else SHARE_MIB + 7,
    )


def gradient_call(
    sizes, up, block, block_act, rows, weights, codes, scales, held, after, last, summed=True
):
    full_shape = (sizes.width, sizes.rows) if up else (sizes.rows, sizes.width)
    half_shape = (sizes.rows // 2, sizes.width)
    kept = weights is not None
    operands = Operands(block)
    operands.add(block_act)
    operands.add(rows)
    if kept and summed:
        operands.add(pltpu.with_memory_space_constraint(weights, pltpu.VMEM))
    elif not kept:
        operands.add(pltpu.with_memory_space_constraint(codes, pltpu.HBM), ANY_SPEC)
        operands.add(scales)
    fresh = held is None
    aliases = {}
    if not fresh:
        at = len(operands.arrays)
        if summed:
            aliases = {at + 1: 2 if last else 1}
            operands.add(held[0])
        else:
            aliases = {at: 0}
        operands.add(pltpu.with_memory_space_constraint(held[1], pltpu.HBM), ANY_SPEC)
        if up:
            operands.add(held[2])
    operands.add(after, ANY_SPEC)
    if not summed:
        outs = []
    elif last:
        outs = [
            (jax.ShapeDtypeStruct(half_shape, jnp.float32), VMEM_SPEC),
            (jax.ShapeDtypeStruct(half_shape, jnp.bfloat16), VMEM_SPEC),
        ]
    else:
        outs = [(jax.ShapeDtypeStruct(full_shape, jnp.float32), VMEM_SPEC)]
    outs.append((pltpu.HBM(codes.shape, jnp.bfloat16), ANY_SPEC))
    if up:
        outs.append((jax.ShapeDtypeStruct((1, sizes.hidden), jnp.float32), VMEM_SPEC))
    piece = sizes.piece(256)
    slot_shape = (sizes.width, piece) if up else (piece, sizes.width)
    slots = min(6, sizes.block_width // piece)
    scratch = [pltpu.VMEM(full_shape, jnp.float32)] if last and summed else []
    scratch += [pltpu.VMEM((slots,) + slot_shape, jnp.bfloat16), pltpu.SemaphoreType.DMA((slots,))]
    if not kept:
        scratch += [
            pltpu.VMEM(sizes.weights_shape(up), jnp.bfloat16),
            pltpu.SemaphoreType.DMA((sizes.block_width // piece,)),
        ]
    return call(
        "up_gradient" if up else "down_gradient",
        functools.partial(gradient_kernel, sizes.side, up, piece, fresh, last, kept, summed),
        operands,
        outs,
        scratch,
        cost_of(sizes.rows, sizes.width, sizes.block_width, 2, 2 if summed else 1),
        GRADIENT_MIB if kept else GRADIENT_MIB + 7,
        aliases,
    )


def activation_call(sizes, sum_in, share, bias):
    block_shape = (sizes.rows, sizes.block_width)
    return pl.pallas_call(
        activation_kernel,
        in_specs=[VMEM_SPEC] * 3,
        out_specs=[VMEM_SPEC] * 2,
        out_shape=[
            jax.ShapeDtypeStruct(block_shape, jnp.bfloat16),
            jax.ShapeDtypeStruct(block_shape, jnp.float32),
        ],
        name="activation",
        compiler_params=pltpu.CompilerParams(vmem_limit_bytes=SHARE_MIB * MIB),
    )(sum_in, share, bias)


def product_call(sizes, block_act, weights, total_in, after):
    half_shape = (sizes.rows // 2, sizes.width)
    return pl.pallas_call(
        product_kernel,
        in_specs=[VMEM_SPEC] * 3 + [ANY_SPEC],
        out_specs=[VMEM_SPEC] * 2,
        out_shape=[
            jax.ShapeDtypeStruct(half_shape, jnp.float32),
            jax.ShapeDtypeStruct(half_shape, jnp.bfloat16),
        ],
        cost_estimate=cost_of(sizes.rows, sizes.width, sizes.block_width, 1, 1),
        name="last_product",
        compiler_params=pltpu.CompilerParams(vmem_limit_bytes=SHARE_MIB * MIB),
    )(block_act, pltpu.with_memory_space_constraint(weights, pltpu.VMEM), total_in, after)


def ring_program(mp_count, hidden_count):
    ring = [(i, (i + 1) % mp_count) for i in range(mp_count)]
    bits = [1 << bit for bit in reversed(range(hidden_count.bit_length() - 1))]

    def partner_pairs(bit):
        return [(i, i ^ bit) for i in range(hidden_count)]

    def after(array, *earlier):
        return lax.optimization_barrier((array, *earlier))[0]

    def first_exchange(own_rows):
        return [own_rows, lax.ppermute(own_rows, "hidden", partner_pairs(bits[0]))]

    def later_exchanges(held, *earlier):
        held = [held[0], after(held[1], *earlier)] if earlier else held
        for bit in bits[1:]:
            held = held + [lax.ppermute(part, "hidden", partner_pairs(bit)) for part in held]
        return held

    def scattered_sum(kept, sent):
        for bit in reversed(bits):
            kept = kept + lax.ppermute(sent, "hidden", partner_pairs(bit)).astype(jnp.float32)
            half = kept.shape[0] // 2
            if bit != bits[0]:
                kept, sent = kept[:half], kept[half:].astype(jnp.bfloat16)
        return kept, sent

    def passed_on(block):
        return lax.ppermute(block, "mp", ring)

    def added(left, right):
        return left.astype(jnp.float32) + right.astype(jnp.float32)

    def on_device(
        tokens, up_codes, up_scales, up_bias, down_codes, down_scales, down_bias, cotangent
    ):
        width, hidden = up_codes.shape
        side = width // up_scales.shape[0]
        block_width = hidden // mp_count
        sizes = Sizes(tokens.shape[0] * hidden_count, width, hidden, block_width, side)
        me = lax.axis_index("mp").astype(jnp.int32)

        up_wide = jnp.repeat(up_scales, side, axis=1)
        down_wide = jnp.repeat(down_scales, side, axis=1).reshape(mp_count, -1, width)
        token_rows = first_exchange(tokens)
        cot_rows = first_exchange(after(cotangent, token_rows[1]))
        token_rows = later_exchanges(token_rows, up_wide, down_wide)

        def block_number(back):
            return ((me + 2 * mp_count - back) % mp_count).reshape(1)

        up_sum = down_sum = None
        up_weights, down_weights = {}, {}
        for back in [*range(1, mp_count), 0]:
            sum_in = up_sum if back else None
            made = share_call(
                sizes, True, block_number(back), token_rows, up_codes, up_wide, sum_in,
                back in KEEP_UP, back == mp_count - 1,
            )
            up_part = made[0]
            if back == mp_count - 1:
                turned_tokens = made[2 if isinstance(token_rows, list) else 1]
            if isinstance(token_rows, list):
                token_rows = made[1]
            if back in KEEP_UP:
                up_weights[back] = made[-1]
            if isinstance(cot_rows, list):
                cot_rows = later_exchanges(cot_rows, up_part)
            sum_in = down_sum if back else None
            made = share_call(
                sizes, False, block_number(back), cot_rows, down_codes, down_wide, sum_in,
                back in KEEP_DOWN,
            )
            down_part = made[0]
            if isinstance(cot_rows, list):
                cot_rows = made[1]
            if back in KEEP_DOWN:
                down_weights[back] = made[-1]
            if back:
                up_sum, down_sum = passed_on(up_part), passed_on(down_part)
        own_bias = lax.dynamic_slice(up_bias.reshape(1, hidden), (0, me * block_width), (1, block_width))
        act_block, slope = activation_call(sizes, up_sum, up_part, own_bias)
        pre_block = (added(down_sum, down_part) * slope).astype(jnp.bfloat16)

        output_held = input_held = None
        for back in range(mp_count):
            last = back == mp_count - 1
            sent_act = act_block if back == 0 else after(act_block, input_held[0])
            next_act = None if last else passed_on(sent_act)
            output_held = gradient_call(
                sizes, False, block_number(back), act_block, cot_rows, down_weights.get(back),
                down_codes, down_wide, output_held,
                pre_block if back == 0 else input_held[0], last,
            )
            sent_pre = pre_block if back == 0 else after(pre_block, output_held[0])
            next_pre = None if last else passed_on(sent_pre)
            if last:
                output_sum, output_sent = scattered_sum(output_held[0], output_held[1])
                tokens_kept, tokens_sent = product_call(
                    sizes, pre_block, up_weights[back], input_held[0], output_held[1]
                )
                tokens_sum, tokens_sent = scattered_sum(tokens_kept, tokens_sent)
                ordering = after(tokens_sent, output_sent)
            else:
                ordering = output_held[0]
            input_held = gradient_call(
                sizes, True, block_number(back), pre_block, turned_tokens, up_weights.get(back),
                up_codes, up_wide, input_held, ordering, last, not last,
            )
            act_block, pre_block = next_act, next_pre
        grad_down = output_held[-1]
        grad_up, grad_up_bias = input_held
        ffn_output = (output_sum + down_bias.astype(jnp.float32)).astype(jnp.bfloat16)
        grad_tokens = tokens_sum.astype(jnp.bfloat16)
        return (ffn_output, grad_tokens, grad_up, grad_down, grad_up_bias.reshape(hidden))

    return on_device


def plain_program(
    tokens, up_codes, up_scales, up_bias, down_codes, down_scales, down_bias, cotangent
):
    w_up = dequantize(up_codes, up_scales)
    w_down = dequantize(down_codes, down_scales)
    cot_rows = lax.all_gather(cotangent, "hidden", axis=0, tiled=True)
    token_rows = lax.all_gather(tokens, "hidden", axis=0, tiled=True)
    bias_up = up_bias.astype(jnp.float32)

    def summed(share, axis):
        return lax.psum_scatter(
            share.astype(jnp.bfloat16), axis, scatter_dimension=0, tiled=True
        ).astype(jnp.float32)

    preact_share = summed(plain_product(token_rows, w_up), "mp") + bias_up
    act_share = gelu_value(preact_share).astype(jnp.bfloat16)
    act_rows = lax.all_gather(act_share, "mp", axis=0, tiled=True)
    grad_share = summed(product_transposed(cot_rows, w_down), "mp")
    grad_pre_share = (grad_share * gelu_slope(preact_share)).astype(jnp.bfloat16)
    grad_pre_rows = lax.all_gather(grad_pre_share, "mp", axis=0, tiled=True)
    output_sum = summed(plain_product(act_rows, w_down), "hidden")
    ffn_output = (output_sum + down_bias.astype(jnp.float32)).astype(jnp.bfloat16)
    grad_tokens = summed(product_transposed(grad_pre_rows, w_up), "hidden").astype(jnp.bfloat16)
    grad_up_bias = jnp.sum(grad_pre_rows, axis=0, dtype=jnp.float32)
    grad_down = transposed_product(act_rows, cot_rows).astype(jnp.bfloat16)
    grad_up = transposed_product(token_rows, grad_pre_rows).astype(jnp.bfloat16)
    return (ffn_output, grad_tokens, grad_up, grad_down, grad_up_bias)


def solution(mesh):
    mp_count, hidden_count = mesh.shape["mp"], mesh.shape["hidden"]

    def on_device(*arrays):
        hidden = arrays[1].shape[1]
        whole_blocks = hidden % (mp_count * LANES) == 0
        if whole_blocks and mp_count > 1 and hidden_count & (hidden_count - 1) == 0:
            return ring_program(mp_count, hidden_count)(*arrays)
        return plain_program(*arrays)

    in_specs = (
        P(("groups", "hidden"), "mp"),
        P("mp", "hidden"),
        P("mp", "hidden"),
        P("hidden"),
        P("hidden", "mp"),
        P("hidden", "mp"),
        P("mp"),
        P(("groups", "hidden"), "mp"),
    )
    out_specs = (
        P(("groups", "hidden"), "mp"),
        P(("groups", "hidden"), "mp"),
        P(("groups", "mp"), "hidden"),
        P(("groups", "hidden"), "mp"),
        P(("groups", "hidden")),
    )
    return jax.shard_map(
        on_device, mesh=mesh, in_specs=in_specs, out_specs=out_specs, check_vma=False
    )
```

```python
import functools

import jax
import jax.numpy as jnp
from jax import lax
from jax.experimental import pallas as pl
from jax.experimental.pallas import tpu as pltpu
from jax.sharding import PartitionSpec as P

root_two_pi = 0.7978845608028654
cubic_coef = 0.044715
LANES = 128
MIB = 1024 * 1024
COST_SCALE = 3
SHARE_MIB = 4
GRADIENT_MIB = 12
DOWN_UNROLL = 3
GRADIENT_UNROLL = 2
KEEP_UP = (0, 3)
KEEP_DOWN = (0, 3)


def gelu_value(argument):
    inner_arg = root_two_pi * (argument + cubic_coef * argument * argument * argument)
    return 0.5 * argument * (1.0 + jnp.tanh(inner_arg))


def gelu_slope(argument):
    inner_arg = root_two_pi * (argument + cubic_coef * argument * argument * argument)
    tangent = jnp.tanh(inner_arg)
    return 0.5 * (1.0 + tangent) + 0.5 * argument * (1.0 - tangent * tangent) * root_two_pi * (
        1.0 + 3.0 * cubic_coef * argument * argument
    )


def dequantize(weight_codes, block_scales):
    row_count, col_count = weight_codes.shape
    scale_rows, scale_cols = block_scales.shape
    blocks = weight_codes.astype(jnp.float32).reshape(
        scale_rows, row_count // scale_rows, scale_cols, col_count // scale_cols
    )
    scaled = blocks * block_scales[:, None, :, None]
    return scaled.reshape(row_count, col_count).astype(jnp.bfloat16)


def plain_product(left_side, right_side):
    return jnp.dot(left_side, right_side, preferred_element_type=jnp.float32)


def product_transposed(left_side, right_side):
    return lax.dot_general(
        left_side, right_side, (((1,), (1,)), ((), ())), preferred_element_type=jnp.float32
    )


def transposed_product(left_side, right_side):
    return lax.dot_general(
        left_side, right_side, (((0,), (0,)), ((), ())), preferred_element_type=jnp.float32
    )


def span(first, count):
    return pl.ds(pl.multiple_of(first, LANES), count)


def up_scaled(side, weights_ref, scales_ref, block, first, count):
    columns = span(first, count)
    scale_columns = span(block * weights_ref.shape[1] + first, count)
    for row in range(weights_ref.shape[0] // side):
        rows = slice(row * side, (row + 1) * side)
        weights_ref[rows, columns] = (
            weights_ref[rows, columns].astype(jnp.float32) * scales_ref[row : row + 1, scale_columns]
        ).astype(jnp.bfloat16)
    return weights_ref[:, columns]


def down_scaled(side, weights_ref, scales_ref, block, first, count):
    for row in range(count // side):
        rows = span(first + row * side, side)
        weights_ref[rows, :] = (
            weights_ref[rows, :].astype(jnp.float32)
            * scales_ref[block, pl.ds(first // side + row, 1), :]
        ).astype(jnp.bfloat16)
    return weights_ref[span(first, count), :]


def code_copy(up, piece, codes_ref, weights_ref, sems, block, index):
    block_width = weights_ref.shape[1 if up else 0]
    there = span(block * block_width + index * piece, piece)
    here = span(index * piece, piece)
    return pltpu.make_async_copy(
        codes_ref.at[:, there] if up else codes_ref.at[there, :],
        weights_ref.at[:, here] if up else weights_ref.at[here, :],
        sems.at[index],
    )


def each(count, body, unroll=1):
    def step(index, nothing):
        body(index)
        return nothing

    lax.fori_loop(0, count, step, None, unroll=unroll)


def share_kernel(side, up, piece, part_count, sum_in, turn, block_ref, *refs):
    refs = list(refs)
    block = block_ref[0]
    parts = [refs.pop(0) for _ in range(part_count)]
    rows_ref = None if part_count else refs.pop(0)
    codes_ref, scales_ref = refs.pop(0), refs.pop(0)
    sum_ref = refs.pop(0) if sum_in else None
    out_ref = refs.pop(0)
    if part_count:
        rows_ref = refs.pop(0)
    turned_ref = refs.pop(0) if turn else None
    weights_ref, sems = refs.pop(0), refs.pop(0)
    sum_held = refs.pop(0) if sum_in else None
    count = out_ref.shape[1] // piece

    def copy(index):
        return code_copy(up, piece, codes_ref, weights_ref, sems, block, index)

    if part_count:
        depth = parts[0].shape[0]
        own_copy = pltpu.make_async_copy(parts[0], rows_ref.at[:depth, :], sems.at[count])
        own_copy.start()
    if sum_in:
        sum_copy = pltpu.make_async_copy(sum_ref, sum_held, sems.at[count])
        sum_copy.start()
    each(count, lambda index: copy(index).start())
    if part_count:
        for index, part in enumerate(parts):
            if index == 0:
                continue
            rows_ref[index * depth : (index + 1) * depth, :] = part[...]
        own_copy.wait()
    if turn:
        turned_ref[...] = rows_ref[...].T
    if sum_in:
        sum_copy.wait()

    def work(index):
        copy(index).wait()
        columns = span(index * piece, piece)
        if up:
            weights = up_scaled(side, weights_ref, scales_ref, block, index * piece, piece)
            share = plain_product(rows_ref[...], weights)
        else:
            weights = down_scaled(side, weights_ref, scales_ref, block, index * piece, piece)
            share = product_transposed(rows_ref[...], weights)
        if sum_in:
            share = share.astype(jnp.bfloat16).astype(jnp.float32) + sum_held[:, columns].astype(
                jnp.float32
            )
        out_ref[:, columns] = share.astype(jnp.bfloat16)

    each(count, work, 1 if up else DOWN_UNROLL)


def activation_kernel(sum_ref, share_ref, bias_ref, act_ref, slope_ref):
    preact = (
        sum_ref[...].astype(jnp.float32)
        + share_ref[...].astype(jnp.float32)
        + bias_ref[...].astype(jnp.float32)
    )
    act_ref[...] = gelu_value(preact).astype(jnp.bfloat16)
    slope_ref[...] = gelu_slope(preact)


def product_kernel(act_ref, weights_ref, total_in, after_ref, kept_ref, sent_ref):
    total = (total_in[...] + product_transposed(weights_ref[...], act_ref[...])).T
    half = total.shape[0] // 2
    kept_ref[...] = total[:half, :]
    sent_ref[...] = total[half:, :].astype(jnp.bfloat16)


def gradient_kernel(side, up, piece, fresh, last, kept_weights, summed, block_ref, *refs):
    refs = list(refs)
    block = block_ref[0]
    block_act, rows_ref = refs.pop(0), refs.pop(0)
    weights_ref = refs.pop(0) if kept_weights and summed else None
    codes_ref, scales_ref = (None, None) if kept_weights else (refs.pop(0), refs.pop(0))
    if not fresh:
        total_in = refs.pop(0) if summed else None
        refs.pop(0)
        bias_in = refs.pop(0) if up else None
    refs.pop(0)
    if last and summed:
        kept_ref, sent_ref = refs.pop(0), refs.pop(0)
    elif summed:
        total_ref = refs.pop(0)
    grad_ref = refs.pop(0)
    bias_ref = refs.pop(0) if up else None
    if last and summed:
        total_ref = refs.pop(0)
    staged, out_sems = refs.pop(0), refs.pop(0)
    block_width = block_act.shape[1]
    count = block_width // piece

    def copy(index):
        return code_copy(up, piece, codes_ref, weights_ref, sems, block, index)

    def write(index):
        there = span(block * block_width + index * piece, piece)
        return pltpu.make_async_copy(
            staged.at[index], grad_ref.at[:, there] if up else grad_ref.at[there, :], out_sems.at[index]
        )

    if not kept_weights:
        weights_ref, sems = refs
        each(count, lambda index: copy(index).start())
    if up and not fresh:
        bias_ref[...] = bias_in[...]
    if summed:
        total_ref[...] = jnp.zeros_like(total_ref) if fresh else total_in[...]

    def work(index):
        columns = span(index * piece, piece)
        act = block_act[:, columns]
        if up:
            gradient = plain_product(rows_ref[...], act)
            bias_ref[0:1, span(block * block_width + index * piece, piece)] = jnp.sum(
                act.astype(jnp.float32), axis=0, keepdims=True
            )
        else:
            gradient = transposed_product(act, rows_ref[...])
        staged[index] = gradient.astype(jnp.bfloat16)
        write(index).start()
        if not summed:
            return
        if not kept_weights:
            copy(index).wait()
            scaled = up_scaled if up else down_scaled
            scaled(side, weights_ref, scales_ref, block, index * piece, piece)
        if up:
            total_ref[...] += product_transposed(weights_ref[:, columns], act)
        else:
            total_ref[...] += plain_product(act, weights_ref[columns, :])

    each(count, work, GRADIENT_UNROLL)
    if last and summed:
        half = total_ref.shape[0] // 2
        kept_ref[...] = total_ref[:half, :]
        sent_ref[...] = total_ref[half:, :].astype(jnp.bfloat16)
    each(count, lambda index: write(index).wait())


def cost_of(token_count, width, hidden_count, products, passes):
    return pl.CostEstimate(
        flops=COST_SCALE * 2 * products * token_count * width * hidden_count,
        bytes_accessed=COST_SCALE * 2 * passes * width * hidden_count,
        transcendentals=0,
    )


ANY_SPEC = pl.BlockSpec(memory_space=pl.ANY)
VMEM_SPEC = pl.BlockSpec(memory_space=pltpu.VMEM)
SMEM_SPEC = pl.BlockSpec(memory_space=pltpu.SMEM)


class Operands:
    def __init__(self, block):
        self.arrays, self.specs = [block], [SMEM_SPEC]

    def add(self, array, spec=VMEM_SPEC):
        self.arrays.append(array)
        self.specs.append(spec)


def call(name, kernel, operands, outs, scratch, cost, limit, aliases=None):
    return pl.pallas_call(
        kernel,
        in_specs=operands.specs,
        out_specs=[spec for _, spec in outs],
        scratch_shapes=scratch,
        out_shape=[shape for shape, _ in outs],
        input_output_aliases=aliases or {},
        cost_estimate=cost,
        name=name,
        compiler_params=pltpu.CompilerParams(vmem_limit_bytes=limit * MIB),
    )(*operands.arrays)


class Sizes:
    def __init__(self, rows, width, hidden, block_width, side):
        self.rows, self.width, self.hidden = rows, width, hidden
        self.block_width, self.side = block_width, side

    def piece(self, most):
        return next(
            size for size in (512, 256, 128) if size <= most and self.block_width % size == 0
        )

    def weights_shape(self, up):
        return (self.width, self.block_width) if up else (self.block_width, self.width)


def share_call(sizes, up, block, rows, codes, scales, sum_in, keep, turn=False):
    parts = rows if isinstance(rows, list) else []
    operands = Operands(block)
    for index, part in enumerate(parts or [rows]):
        if parts and index == 0:
            operands.add(pltpu.with_memory_space_constraint(part, pltpu.HBM), ANY_SPEC)
        else:
            operands.add(part)
    operands.add(pltpu.with_memory_space_constraint(codes, pltpu.HBM), ANY_SPEC)
    operands.add(scales)
    if sum_in is not None:
        operands.add(sum_in, ANY_SPEC)
    outs = [(pltpu.VMEM((sizes.rows, sizes.block_width), jnp.bfloat16), VMEM_SPEC)]
    if parts:
        outs.append((jax.ShapeDtypeStruct((sizes.rows, sizes.width), jnp.bfloat16), VMEM_SPEC))
    if turn:
        outs.append((jax.ShapeDtypeStruct((sizes.width, sizes.rows), jnp.bfloat16), VMEM_SPEC))
    weights = pltpu.VMEM(sizes.weights_shape(up), jnp.bfloat16)
    if keep:
        outs.append((weights, VMEM_SPEC))
    piece = sizes.piece(256 if up else 512)
    return call(
        "up_share" if up else "down_share",
        functools.partial(share_kernel, sizes.side, up, piece, len(parts), sum_in is not None, turn),
        operands,
        outs,
        ([] if keep else [weights])
        + [pltpu.SemaphoreType.DMA((sizes.block_width // piece + 1,))]
        + ([] if sum_in is None else [pltpu.VMEM((sizes.rows, sizes.block_width), jnp.bfloat16)]),
        cost_of(sizes.rows, sizes.width, sizes.block_width, 1, 1),
        SHARE_MIB if keep else SHARE_MIB + 7,
    )


def gradient_call(
    sizes, up, block, block_act, rows, weights, codes, scales, held, after, last, summed=True
):
    full_shape = (sizes.width, sizes.rows) if up else (sizes.rows, sizes.width)
    half_shape = (sizes.rows // 2, sizes.width)
    kept = weights is not None
    operands = Operands(block)
    operands.add(block_act)
    operands.add(rows)
    if kept and summed:
        operands.add(pltpu.with_memory_space_constraint(weights, pltpu.VMEM))
    elif not kept:
        operands.add(pltpu.with_memory_space_constraint(codes, pltpu.HBM), ANY_SPEC)
        operands.add(scales)
    fresh = held is None
    aliases = {}
    if not fresh:
        at = len(operands.arrays)
        if summed:
            aliases = {at + 1: 2 if last else 1}
            operands.add(held[0])
        else:
            aliases = {at: 0}
        operands.add(pltpu.with_memory_space_constraint(held[1], pltpu.HBM), ANY_SPEC)
        if up:
            operands.add(held[2])
    operands.add(after, ANY_SPEC)
    if not summed:
        outs = []
    elif last:
        outs = [
            (jax.ShapeDtypeStruct(half_shape, jnp.float32), VMEM_SPEC),
            (jax.ShapeDtypeStruct(half_shape, jnp.bfloat16), VMEM_SPEC),
        ]
    else:
        outs = [(jax.ShapeDtypeStruct(full_shape, jnp.float32), VMEM_SPEC)]
    outs.append((pltpu.HBM(codes.shape, jnp.bfloat16), ANY_SPEC))
    if up:
        outs.append((jax.ShapeDtypeStruct((1, sizes.hidden), jnp.float32), VMEM_SPEC))
    piece = sizes.piece(256)
    slot_shape = (sizes.width, piece) if up else (piece, sizes.width)
    slots = sizes.block_width // piece
    scratch = [pltpu.VMEM(full_shape, jnp.float32)] if last and summed else []
    scratch += [pltpu.VMEM((slots,) + slot_shape, jnp.bfloat16), pltpu.SemaphoreType.DMA((slots,))]
    if not kept:
        scratch += [
            pltpu.VMEM(sizes.weights_shape(up), jnp.bfloat16),
            pltpu.SemaphoreType.DMA((sizes.block_width // piece,)),
        ]
    return call(
        "up_gradient" if up else "down_gradient",
        functools.partial(gradient_kernel, sizes.side, up, piece, fresh, last, kept, summed),
        operands,
        outs,
        scratch,
        cost_of(sizes.rows, sizes.width, sizes.block_width, 2, 2 if summed else 1),
        GRADIENT_MIB if kept else GRADIENT_MIB + 7,
        aliases,
    )


def activation_call(sizes, sum_in, share, bias):
    block_shape = (sizes.rows, sizes.block_width)
    return pl.pallas_call(
        activation_kernel,
        in_specs=[VMEM_SPEC] * 3,
        out_specs=[VMEM_SPEC] * 2,
        out_shape=[
            jax.ShapeDtypeStruct(block_shape, jnp.bfloat16),
            jax.ShapeDtypeStruct(block_shape, jnp.float32),
        ],
        name="activation",
        compiler_params=pltpu.CompilerParams(vmem_limit_bytes=SHARE_MIB * MIB),
    )(sum_in, share, bias)


def product_call(sizes, block_act, weights, total_in, after):
    half_shape = (sizes.rows // 2, sizes.width)
    return pl.pallas_call(
        product_kernel,
        in_specs=[VMEM_SPEC] * 3 + [ANY_SPEC],
        out_specs=[VMEM_SPEC] * 2,
        out_shape=[
            jax.ShapeDtypeStruct(half_shape, jnp.float32),
            jax.ShapeDtypeStruct(half_shape, jnp.bfloat16),
        ],
        cost_estimate=cost_of(sizes.rows, sizes.width, sizes.block_width, 1, 1),
        name="last_product",
        compiler_params=pltpu.CompilerParams(vmem_limit_bytes=SHARE_MIB * MIB),
    )(block_act, pltpu.with_memory_space_constraint(weights, pltpu.VMEM), total_in, after)


def ring_program(mp_count, hidden_count):
    ring = [(i, (i + 1) % mp_count) for i in range(mp_count)]
    bits = [1 << bit for bit in reversed(range(hidden_count.bit_length() - 1))]

    def partner_pairs(bit):
        return [(i, i ^ bit) for i in range(hidden_count)]

    def after(array, *earlier):
        return lax.optimization_barrier((array, *earlier))[0]

    def first_exchange(own_rows):
        return [own_rows, lax.ppermute(own_rows, "hidden", partner_pairs(bits[0]))]

    def later_exchanges(held, *earlier):
        held = [held[0], after(held[1], *earlier)] if earlier else held
        for bit in bits[1:]:
            held = held + [lax.ppermute(part, "hidden", partner_pairs(bit)) for part in held]
        return held

    def scattered_sum(kept, sent):
        for bit in reversed(bits):
            kept = kept + lax.ppermute(sent, "hidden", partner_pairs(bit)).astype(jnp.float32)
            half = kept.shape[0] // 2
            if bit != bits[0]:
                kept, sent = kept[:half], kept[half:].astype(jnp.bfloat16)
        return kept, sent

    def passed_on(block):
        return lax.ppermute(block, "mp", ring)

    def added(left, right):
        return left.astype(jnp.float32) + right.astype(jnp.float32)

    def on_device(
        tokens, up_codes, up_scales, up_bias, down_codes, down_scales, down_bias, cotangent
    ):
        width, hidden = up_codes.shape
        side = width // up_scales.shape[0]
        block_width = hidden // mp_count
        sizes = Sizes(tokens.shape[0] * hidden_count, width, hidden, block_width, side)
        me = lax.axis_index("mp").astype(jnp.int32)

        up_wide = jnp.repeat(up_scales, side, axis=1)
        down_wide = jnp.repeat(down_scales, side, axis=1).reshape(mp_count, -1, width)
        token_rows = first_exchange(tokens)
        cot_rows = first_exchange(after(cotangent, token_rows[1]))
        own_bias = lax.dynamic_slice(
            up_bias.reshape(1, hidden), (0, me * block_width), (1, block_width)
        )
        token_rows = later_exchanges(token_rows, up_wide, down_wide, own_bias)

        def block_number(back):
            return ((me + 2 * mp_count - back) % mp_count).reshape(1)

        up_weights, down_weights = {}, {}

        def up_share(back, rows, sum_in, turn, *earlier):
            block = after(block_number(back), *earlier)
            made = share_call(
                sizes, True, block, rows, up_codes, up_wide, sum_in, back in KEEP_UP, turn
            )
            if back in KEEP_UP:
                up_weights[back] = made[-1]
            return made

        def down_share(back, rows, sum_in, *earlier):
            block = after(block_number(back), *earlier)
            made = share_call(
                sizes, False, block, rows, down_codes, down_wide, sum_in, back in KEEP_DOWN
            )
            if back in KEEP_DOWN:
                down_weights[back] = made[-1]
            return made

        up_part, token_rows, *made = up_share(1, token_rows, None, mp_count == 2)
        turned_tokens = made[0] if mp_count == 2 else None
        up_sum = passed_on(up_part)
        down_part, cot_rows, *_ = down_share(1, later_exchanges(cot_rows, up_part), None)
        down_sum = passed_on(down_part)
        for back in range(2, mp_count):
            last = back == mp_count - 1
            up_part, *made = up_share(back, token_rows, up_sum, last)
            up_sum = passed_on(up_part)
            if last:
                turned_tokens = made[0]
                own_part = up_share(0, token_rows, None, False, up_part)[0]
            down_part = down_share(back, cot_rows, down_sum, *([own_part] if last else []))[0]
            down_sum = passed_on(down_part)
        if mp_count == 2:
            own_part = up_share(0, token_rows, None, False, up_part)[0]
        act_block, slope = activation_call(sizes, up_sum, own_part, own_bias)
        down_part = down_share(0, cot_rows, None, act_block)[0]
        pre_block = (added(down_sum, down_part) * slope).astype(jnp.bfloat16)

        output_held = input_held = None
        for back in range(mp_count):
            last = back == mp_count - 1
            sent_act = act_block if back == 0 else after(act_block, input_held[0])
            next_act = None if last else passed_on(sent_act)
            output_held = gradient_call(
                sizes, False, block_number(back), act_block, cot_rows, down_weights.get(back),
                down_codes, down_wide, output_held,
                pre_block if back == 0 else input_held[0], last,
            )
            sent_pre = pre_block if back == 0 else after(pre_block, output_held[0])
            next_pre = None if last else passed_on(sent_pre)
            if last:
                output_sum, output_sent = scattered_sum(output_held[0], output_held[1])
                tokens_kept, tokens_sent = product_call(
                    sizes, pre_block, up_weights[back], input_held[0], output_held[1]
                )
                tokens_sum, tokens_sent = scattered_sum(tokens_kept, tokens_sent)
                ordering = after(tokens_sent, output_sent)
            else:
                ordering = output_held[0]
            input_held = gradient_call(
                sizes, True, block_number(back), pre_block, turned_tokens, up_weights.get(back),
                up_codes, up_wide, input_held, ordering, last, not last,
            )
            act_block, pre_block = next_act, next_pre
        grad_down = output_held[-1]
        grad_up, grad_up_bias = input_held
        ffn_output = (output_sum + down_bias.astype(jnp.float32)).astype(jnp.bfloat16)
        grad_tokens = tokens_sum.astype(jnp.bfloat16)
        return (ffn_output, grad_tokens, grad_up, grad_down, grad_up_bias.reshape(hidden))

    return on_device


def plain_program(
    tokens, up_codes, up_scales, up_bias, down_codes, down_scales, down_bias, cotangent
):
    w_up = dequantize(up_codes, up_scales)
    w_down = dequantize(down_codes, down_scales)
    cot_rows = lax.all_gather(cotangent, "hidden", axis=0, tiled=True)
    token_rows = lax.all_gather(tokens, "hidden", axis=0, tiled=True)
    bias_up = up_bias.astype(jnp.float32)

    def summed(share, axis):
        return lax.psum_scatter(
            share.astype(jnp.bfloat16), axis, scatter_dimension=0, tiled=True
        ).astype(jnp.float32)

    preact_share = summed(plain_product(token_rows, w_up), "mp") + bias_up
    act_share = gelu_value(preact_share).astype(jnp.bfloat16)
    act_rows = lax.all_gather(act_share, "mp", axis=0, tiled=True)
    grad_share = summed(product_transposed(cot_rows, w_down), "mp")
    grad_pre_share = (grad_share * gelu_slope(preact_share)).astype(jnp.bfloat16)
    grad_pre_rows = lax.all_gather(grad_pre_share, "mp", axis=0, tiled=True)
    output_sum = summed(plain_product(act_rows, w_down), "hidden")
    ffn_output = (output_sum + down_bias.astype(jnp.float32)).astype(jnp.bfloat16)
    grad_tokens = summed(product_transposed(grad_pre_rows, w_up), "hidden").astype(jnp.bfloat16)
    grad_up_bias = jnp.sum(grad_pre_rows, axis=0, dtype=jnp.float32)
    grad_down = transposed_product(act_rows, cot_rows).astype(jnp.bfloat16)
    grad_up = transposed_product(token_rows, grad_pre_rows).astype(jnp.bfloat16)
    return (ffn_output, grad_tokens, grad_up, grad_down, grad_up_bias)


def solution(mesh):
    mp_count, hidden_count = mesh.shape["mp"], mesh.shape["hidden"]

    def on_device(*arrays):
        hidden = arrays[1].shape[1]
        whole_blocks = hidden % (mp_count * LANES) == 0
        if whole_blocks and mp_count > 1 and hidden_count & (hidden_count - 1) == 0:
            return ring_program(mp_count, hidden_count)(*arrays)
        return plain_program(*arrays)

    in_specs = (
        P(("groups", "hidden"), "mp"),
        P("mp", "hidden"),
        P("mp", "hidden"),
        P("hidden"),
        P("hidden", "mp"),
        P("hidden", "mp"),
        P("mp"),
        P(("groups", "hidden"), "mp"),
    )
    out_specs = (
        P(("groups", "hidden"), "mp"),
        P(("groups", "hidden"), "mp"),
        P(("groups", "mp"), "hidden"),
        P(("groups", "hidden"), "mp"),
        P(("groups", "hidden")),
    )
    return jax.shard_map(
        on_device, mesh=mesh, in_specs=in_specs, out_specs=out_specs, check_vma=False
    )
```

```python
import functools

import jax
import jax.numpy as jnp
from jax import lax
from jax.experimental import pallas as pl
from jax.experimental.pallas import tpu as pltpu
from jax.sharding import PartitionSpec as P

root_two_pi = 0.7978845608028654
cubic_coef = 0.044715
LANES = 128
MIB = 1024 * 1024
SHARE_COST = 3
GRADIENT_COST = 3
SHARE_MIB = 4
GRADIENT_MIB = 12
DOWN_UNROLL = 3
GRADIENT_UNROLL = 2
KEEP_UP = (0, 3)
KEEP_DOWN = (0, 3)


def gelu_value(argument):
    inner_arg = root_two_pi * (argument + cubic_coef * argument * argument * argument)
    return 0.5 * argument * (1.0 + jnp.tanh(inner_arg))


def gelu_slope(argument):
    inner_arg = root_two_pi * (argument + cubic_coef * argument * argument * argument)
    tangent = jnp.tanh(inner_arg)
    return 0.5 * (1.0 + tangent) + 0.5 * argument * (1.0 - tangent * tangent) * root_two_pi * (
        1.0 + 3.0 * cubic_coef * argument * argument
    )


def dequantize(weight_codes, block_scales):
    row_count, col_count = weight_codes.shape
    scale_rows, scale_cols = block_scales.shape
    blocks = weight_codes.astype(jnp.float32).reshape(
        scale_rows, row_count // scale_rows, scale_cols, col_count // scale_cols
    )
    scaled = blocks * block_scales[:, None, :, None]
    return scaled.reshape(row_count, col_count).astype(jnp.bfloat16)


def plain_product(left_side, right_side):
    return jnp.dot(left_side, right_side, preferred_element_type=jnp.float32)


def product_transposed(left_side, right_side):
    return lax.dot_general(
        left_side, right_side, (((1,), (1,)), ((), ())), preferred_element_type=jnp.float32
    )


def transposed_product(left_side, right_side):
    return lax.dot_general(
        left_side, right_side, (((0,), (0,)), ((), ())), preferred_element_type=jnp.float32
    )


def span(first, count):
    return pl.ds(pl.multiple_of(first, LANES), count)


def up_scaled(side, weights_ref, scales_ref, block, first, count):
    columns = span(first, count)
    scale_columns = span(block * weights_ref.shape[1] + first, count)
    for row in range(weights_ref.shape[0] // side):
        rows = slice(row * side, (row + 1) * side)
        weights_ref[rows, columns] = (
            weights_ref[rows, columns].astype(jnp.float32) * scales_ref[row : row + 1, scale_columns]
        ).astype(jnp.bfloat16)
    return weights_ref[:, columns]


def down_scaled(side, weights_ref, scales_ref, block, first, count):
    for row in range(count // side):
        rows = span(first + row * side, side)
        weights_ref[rows, :] = (
            weights_ref[rows, :].astype(jnp.float32)
            * scales_ref[block, pl.ds(first // side + row, 1), :]
        ).astype(jnp.bfloat16)
    return weights_ref[span(first, count), :]


def code_copy(up, piece, codes_ref, weights_ref, sems, block, index):
    block_width = weights_ref.shape[1 if up else 0]
    there = span(block * block_width + index * piece, piece)
    here = span(index * piece, piece)
    return pltpu.make_async_copy(
        codes_ref.at[:, there] if up else codes_ref.at[there, :],
        weights_ref.at[:, here] if up else weights_ref.at[here, :],
        sems.at[index],
    )


def each(count, body, unroll=1):
    def step(index, nothing):
        body(index)
        return nothing

    lax.fori_loop(0, count, step, None, unroll=unroll)


def share_kernel(side, up, piece, part_count, sum_in, turn, block_ref, *refs):
    refs = list(refs)
    block = block_ref[0]
    parts = [refs.pop(0) for _ in range(part_count)]
    rows_ref = None if part_count else refs.pop(0)
    codes_ref, scales_ref = refs.pop(0), refs.pop(0)
    sum_ref = refs.pop(0) if sum_in else None
    out_ref = refs.pop(0)
    if part_count:
        rows_ref = refs.pop(0)
    turned_ref = refs.pop(0) if turn else None
    weights_ref, sems = refs.pop(0), refs.pop(0)
    sum_held = refs.pop(0) if sum_in else None
    count = out_ref.shape[1] // piece

    def copy(index):
        return code_copy(up, piece, codes_ref, weights_ref, sems, block, index)

    if part_count:
        depth = parts[0].shape[0]
        own_copy = pltpu.make_async_copy(parts[0], rows_ref.at[:depth, :], sems.at[count])
        own_copy.start()
    if sum_in:
        sum_copy = pltpu.make_async_copy(sum_ref, sum_held, sems.at[count])
        sum_copy.start()
    each(count, lambda index: copy(index).start())
    if part_count:
        for index, part in enumerate(parts):
            if index == 0:
                continue
            rows_ref[index * depth : (index + 1) * depth, :] = part[...]
        own_copy.wait()
    if turn:
        turned_ref[...] = rows_ref[...].T
    if sum_in:
        sum_copy.wait()

    def work(index):
        copy(index).wait()
        columns = span(index * piece, piece)
        if up:
            weights = up_scaled(side, weights_ref, scales_ref, block, index * piece, piece)
            share = plain_product(rows_ref[...], weights)
        else:
            weights = down_scaled(side, weights_ref, scales_ref, block, index * piece, piece)
            share = product_transposed(rows_ref[...], weights)
        if sum_in:
            share = share.astype(jnp.bfloat16).astype(jnp.float32) + sum_held[:, columns].astype(
                jnp.float32
            )
        out_ref[:, columns] = share.astype(jnp.bfloat16)

    each(count, work, 1 if up else DOWN_UNROLL)


def activation_kernel(sum_ref, share_ref, bias_ref, act_ref, slope_ref):
    preact = (
        sum_ref[...].astype(jnp.float32)
        + share_ref[...].astype(jnp.float32)
        + bias_ref[...].astype(jnp.float32)
    )
    act_ref[...] = gelu_value(preact).astype(jnp.bfloat16)
    slope_ref[...] = gelu_slope(preact)


def product_kernel(act_ref, weights_ref, total_in, after_ref, kept_ref, sent_ref):
    total = (total_in[...] + product_transposed(weights_ref[...], act_ref[...])).T
    half = total.shape[0] // 2
    kept_ref[...] = total[:half, :]
    sent_ref[...] = total[half:, :].astype(jnp.bfloat16)


def gradient_kernel(side, up, piece, fresh, last, kept_weights, summed, block_ref, *refs):
    refs = list(refs)
    block = block_ref[0]
    block_act, rows_ref = refs.pop(0), refs.pop(0)
    weights_ref = refs.pop(0) if kept_weights and summed else None
    codes_ref, scales_ref = (None, None) if kept_weights else (refs.pop(0), refs.pop(0))
    if not fresh:
        total_in = refs.pop(0) if summed else None
        refs.pop(0)
        bias_in = refs.pop(0) if up else None
    refs.pop(0)
    if last and summed:
        kept_ref, sent_ref = refs.pop(0), refs.pop(0)
    elif summed:
        total_ref = refs.pop(0)
    grad_ref = refs.pop(0)
    bias_ref = refs.pop(0) if up else None
    if last and summed:
        total_ref = refs.pop(0)
    staged, out_sems = refs.pop(0), refs.pop(0)
    block_width = block_act.shape[1]
    count = block_width // piece

    def copy(index):
        return code_copy(up, piece, codes_ref, weights_ref, sems, block, index)

    def write(index):
        there = span(block * block_width + index * piece, piece)
        return pltpu.make_async_copy(
            staged.at[index], grad_ref.at[:, there] if up else grad_ref.at[there, :], out_sems.at[index]
        )

    if not kept_weights:
        weights_ref, sems = refs
        each(count, lambda index: copy(index).start())
    if up and not fresh:
        bias_ref[...] = bias_in[...]
    if summed:
        total_ref[...] = jnp.zeros_like(total_ref) if fresh else total_in[...]

    def work(index):
        columns = span(index * piece, piece)
        act = block_act[:, columns]
        if summed and not kept_weights:
            copy(index).wait()
            scaled = up_scaled if up else down_scaled
            scaled(side, weights_ref, scales_ref, block, index * piece, piece)
        if up:
            gradient = plain_product(rows_ref[...], act)
            bias_ref[0:1, span(block * block_width + index * piece, piece)] = jnp.sum(
                act.astype(jnp.float32), axis=0, keepdims=True
            )
        else:
            gradient = transposed_product(act, rows_ref[...])
        staged[index] = gradient.astype(jnp.bfloat16)
        if summed and up:
            total_ref[...] += product_transposed(weights_ref[:, columns], act)
        elif summed:
            total_ref[...] += plain_product(act, weights_ref[columns, :])
        write(index).start()

    each(count, work, GRADIENT_UNROLL)
    if last and summed:
        half = total_ref.shape[0] // 2
        kept_ref[...] = total_ref[:half, :]
        sent_ref[...] = total_ref[half:, :].astype(jnp.bfloat16)
    each(count, lambda index: write(index).wait())


def cost_of(scale, token_count, width, hidden_count, products, passes):
    return pl.CostEstimate(
        flops=int(scale * 2 * products * token_count * width * hidden_count),
        bytes_accessed=int(scale * 2 * passes * width * hidden_count),
        transcendentals=0,
    )


ANY_SPEC = pl.BlockSpec(memory_space=pl.ANY)
VMEM_SPEC = pl.BlockSpec(memory_space=pltpu.VMEM)
SMEM_SPEC = pl.BlockSpec(memory_space=pltpu.SMEM)


class Operands:
    def __init__(self, block):
        self.arrays, self.specs = [block], [SMEM_SPEC]

    def add(self, array, spec=VMEM_SPEC):
        self.arrays.append(array)
        self.specs.append(spec)


def call(name, kernel, operands, outs, scratch, cost, limit, aliases=None):
    return pl.pallas_call(
        kernel,
        in_specs=operands.specs,
        out_specs=[spec for _, spec in outs],
        scratch_shapes=scratch,
        out_shape=[shape for shape, _ in outs],
        input_output_aliases=aliases or {},
        cost_estimate=cost,
        name=name,
        compiler_params=pltpu.CompilerParams(vmem_limit_bytes=limit * MIB),
    )(*operands.arrays)


class Sizes:
    def __init__(self, rows, width, hidden, block_width, side):
        self.rows, self.width, self.hidden = rows, width, hidden
        self.block_width, self.side = block_width, side

    def piece(self, most):
        return next(
            size for size in (512, 256, 128) if size <= most and self.block_width % size == 0
        )

    def weights_shape(self, up):
        return (self.width, self.block_width) if up else (self.block_width, self.width)


def share_call(sizes, up, block, rows, codes, scales, sum_in, keep, turn=False):
    parts = rows if isinstance(rows, list) else []
    operands = Operands(block)
    for index, part in enumerate(parts or [rows]):
        if parts and index == 0:
            operands.add(pltpu.with_memory_space_constraint(part, pltpu.HBM), ANY_SPEC)
        else:
            operands.add(part)
    operands.add(pltpu.with_memory_space_constraint(codes, pltpu.HBM), ANY_SPEC)
    operands.add(scales)
    if sum_in is not None:
        operands.add(sum_in, ANY_SPEC)
    outs = [(pltpu.VMEM((sizes.rows, sizes.block_width), jnp.bfloat16), VMEM_SPEC)]
    if parts:
        outs.append((jax.ShapeDtypeStruct((sizes.rows, sizes.width), jnp.bfloat16), VMEM_SPEC))
    if turn:
        outs.append((jax.ShapeDtypeStruct((sizes.width, sizes.rows), jnp.bfloat16), VMEM_SPEC))
    weights = pltpu.VMEM(sizes.weights_shape(up), jnp.bfloat16)
    if keep:
        outs.append((weights, VMEM_SPEC))
    piece = sizes.piece(256 if up else 512)
    return call(
        "up_share" if up else "down_share",
        functools.partial(share_kernel, sizes.side, up, piece, len(parts), sum_in is not None, turn),
        operands,
        outs,
        ([] if keep else [weights])
        + [pltpu.SemaphoreType.DMA((sizes.block_width // piece + 1,))]
        + ([] if sum_in is None else [pltpu.VMEM((sizes.rows, sizes.block_width), jnp.bfloat16)]),
        cost_of(SHARE_COST, sizes.rows, sizes.width, sizes.block_width, 1, 1),
        SHARE_MIB if keep else SHARE_MIB + 7,
    )


def gradient_call(
    sizes, up, block, block_act, rows, weights, codes, scales, held, after, last, summed=True
):
    full_shape = (sizes.width, sizes.rows) if up else (sizes.rows, sizes.width)
    half_shape = (sizes.rows // 2, sizes.width)
    kept = weights is not None
    operands = Operands(block)
    operands.add(block_act)
    operands.add(rows)
    if kept and summed:
        operands.add(pltpu.with_memory_space_constraint(weights, pltpu.VMEM))
    elif not kept:
        operands.add(pltpu.with_memory_space_constraint(codes, pltpu.HBM), ANY_SPEC)
        operands.add(scales)
    fresh = held is None
    aliases = {}
    if not fresh:
        at = len(operands.arrays)
        if summed:
            aliases = {at + 1: 2 if last else 1}
            operands.add(held[0])
        else:
            aliases = {at: 0}
        operands.add(pltpu.with_memory_space_constraint(held[1], pltpu.HBM), ANY_SPEC)
        if up:
            operands.add(held[2])
    operands.add(after, ANY_SPEC)
    if not summed:
        outs = []
    elif last:
        outs = [
            (jax.ShapeDtypeStruct(half_shape, jnp.float32), VMEM_SPEC),
            (jax.ShapeDtypeStruct(half_shape, jnp.bfloat16), VMEM_SPEC),
        ]
    else:
        outs = [(jax.ShapeDtypeStruct(full_shape, jnp.float32), VMEM_SPEC)]
    outs.append((pltpu.HBM(codes.shape, jnp.bfloat16), ANY_SPEC))
    if up:
        outs.append((jax.ShapeDtypeStruct((1, sizes.hidden), jnp.float32), VMEM_SPEC))
    piece = sizes.piece(256)
    slot_shape = (sizes.width, piece) if up else (piece, sizes.width)
    slots = sizes.block_width // piece
    scratch = [pltpu.VMEM(full_shape, jnp.float32)] if last and summed else []
    scratch += [pltpu.VMEM((slots,) + slot_shape, jnp.bfloat16), pltpu.SemaphoreType.DMA((slots,))]
    if not kept:
        scratch += [
            pltpu.VMEM(sizes.weights_shape(up), jnp.bfloat16),
            pltpu.SemaphoreType.DMA((sizes.block_width // piece,)),
        ]
    return call(
        "up_gradient" if up else "down_gradient",
        functools.partial(gradient_kernel, sizes.side, up, piece, fresh, last, kept, summed),
        operands,
        outs,
        scratch,
        cost_of(GRADIENT_COST, sizes.rows, sizes.width, sizes.block_width, 2, 2 if summed else 1),
        GRADIENT_MIB if kept else GRADIENT_MIB + 7,
        aliases,
    )


def activation_call(sizes, sum_in, share, bias):
    block_shape = (sizes.rows, sizes.block_width)
    return pl.pallas_call(
        activation_kernel,
        in_specs=[VMEM_SPEC] * 3,
        out_specs=[VMEM_SPEC] * 2,
        out_shape=[
            jax.ShapeDtypeStruct(block_shape, jnp.bfloat16),
            jax.ShapeDtypeStruct(block_shape, jnp.float32),
        ],
        name="activation",
        compiler_params=pltpu.CompilerParams(vmem_limit_bytes=SHARE_MIB * MIB),
    )(sum_in, share, bias)


def product_call(sizes, block_act, weights, total_in, after):
    half_shape = (sizes.rows // 2, sizes.width)
    return pl.pallas_call(
        product_kernel,
        in_specs=[VMEM_SPEC] * 3 + [ANY_SPEC],
        out_specs=[VMEM_SPEC] * 2,
        out_shape=[
            jax.ShapeDtypeStruct(half_shape, jnp.float32),
            jax.ShapeDtypeStruct(half_shape, jnp.bfloat16),
        ],
        cost_estimate=cost_of(SHARE_COST, sizes.rows, sizes.width, sizes.block_width, 1, 1),
        name="last_product",
        compiler_params=pltpu.CompilerParams(vmem_limit_bytes=SHARE_MIB * MIB),
    )(block_act, pltpu.with_memory_space_constraint(weights, pltpu.VMEM), total_in, after)


def ring_program(mp_count, hidden_count):
    order = [0, *range(1, mp_count, 2), *reversed(range(2, mp_count, 2))]
    ring = [(order[i], order[(i + 1) % mp_count]) for i in range(mp_count)]
    bits = [1 << bit for bit in reversed(range(hidden_count.bit_length() - 1))]

    def partner_pairs(bit):
        return [(i, i ^ bit) for i in range(hidden_count)]

    def after(array, *earlier):
        return lax.optimization_barrier((array, *earlier))[0]

    def first_exchange(own_rows):
        return [own_rows, lax.ppermute(own_rows, "hidden", partner_pairs(bits[0]))]

    def later_exchanges(held, *earlier):
        held = [held[0], after(held[1], *earlier)] if earlier else held
        for bit in bits[1:]:
            held = held + [lax.ppermute(part, "hidden", partner_pairs(bit)) for part in held]
        return held

    def scattered_sum(kept, sent):
        for bit in reversed(bits):
            kept = kept + lax.ppermute(sent, "hidden", partner_pairs(bit)).astype(jnp.float32)
            half = kept.shape[0] // 2
            if bit != bits[0]:
                kept, sent = kept[:half], kept[half:].astype(jnp.bfloat16)
        return kept, sent

    def passed_on(block):
        return lax.ppermute(block, "mp", ring)

    def added(left, right):
        return left.astype(jnp.float32) + right.astype(jnp.float32)

    def on_device(
        tokens, up_codes, up_scales, up_bias, down_codes, down_scales, down_bias, cotangent
    ):
        width, hidden = up_codes.shape
        side = width // up_scales.shape[0]
        block_width = hidden // mp_count
        sizes = Sizes(tokens.shape[0] * hidden_count, width, hidden, block_width, side)
        index = lax.axis_index("mp").astype(jnp.int32)
        me = jnp.where(index % 2 == 1, (index + 1) // 2, (mp_count - index // 2) % mp_count)

        up_wide = jnp.repeat(up_scales, side, axis=1)
        down_wide = jnp.repeat(down_scales, side, axis=1).reshape(mp_count, -1, width)
        own_bias = lax.dynamic_slice(
            up_bias.reshape(1, hidden), (0, me * block_width), (1, block_width)
        )
        token_rows = first_exchange(tokens)
        cot_rows = first_exchange(after(cotangent, up_wide, down_wide, own_bias))
        token_rows = later_exchanges(token_rows, up_wide, down_wide, own_bias)

        def block_number(back):
            return ((me + 2 * mp_count - back) % mp_count).reshape(1)

        up_weights, down_weights = {}, {}

        def up_share(back, rows, sum_in, turn, *earlier):
            block = after(block_number(back), *earlier)
            made = share_call(
                sizes, True, block, rows, up_codes, up_wide, sum_in, back in KEEP_UP, turn
            )
            if back in KEEP_UP:
                up_weights[back] = made[-1]
            return made

        def down_share(back, rows, sum_in, *earlier):
            block = after(block_number(back), *earlier)
            made = share_call(
                sizes, False, block, rows, down_codes, down_wide, sum_in, back in KEEP_DOWN
            )
            if back in KEEP_DOWN:
                down_weights[back] = made[-1]
            return made

        up_part, token_rows, *made = up_share(1, token_rows, None, mp_count == 2)
        turned_tokens = made[0] if mp_count == 2 else None
        up_sum = passed_on(up_part)
        down_part, cot_rows, *_ = down_share(1, later_exchanges(cot_rows, up_part), None)
        down_sum = passed_on(down_part)
        for back in range(2, mp_count):
            last = back == mp_count - 1
            up_part, *made = up_share(back, token_rows, up_sum, last)
            up_sum = passed_on(up_part)
            if last:
                turned_tokens = made[0]
                own_part = up_share(0, token_rows, None, False, up_part)[0]
            down_part = down_share(back, cot_rows, down_sum, *([own_part] if last else []))[0]
            down_sum = passed_on(down_part)
        if mp_count == 2:
            own_part = up_share(0, token_rows, None, False, up_part)[0]
        act_block, slope = activation_call(sizes, up_sum, own_part, own_bias)
        down_part = down_share(0, cot_rows, None, act_block)[0]
        pre_block = (added(down_sum, down_part) * slope).astype(jnp.bfloat16)

        output_held = input_held = None
        for back in range(mp_count):
            last = back == mp_count - 1
            sent_act = act_block if back == 0 else after(act_block, output_held[0])
            next_act = None if last else passed_on(sent_act)
            sent_pre = pre_block if back == 0 else after(pre_block, input_held[0])
            next_pre = None if last else passed_on(sent_pre)
            output_held = gradient_call(
                sizes, False, block_number(back), act_block, cot_rows, down_weights.get(back),
                down_codes, down_wide, output_held,
                pre_block if back == 0 else input_held[0], last,
            )
            if last:
                output_sum, output_sent = scattered_sum(output_held[0], output_held[1])
                tokens_kept, tokens_sent = product_call(
                    sizes, pre_block, up_weights[back], input_held[0], output_held[1]
                )
                tokens_sum, tokens_sent = scattered_sum(tokens_kept, tokens_sent)
                ordering = after(tokens_sent, output_sent)
            else:
                ordering = output_held[0]
            input_held = gradient_call(
                sizes, True, block_number(back), pre_block, turned_tokens, up_weights.get(back),
                up_codes, up_wide, input_held, ordering, last, not last,
            )
            act_block, pre_block = next_act, next_pre
        grad_down = output_held[-1]
        grad_up, grad_up_bias = input_held
        ffn_output = (output_sum + down_bias.astype(jnp.float32)).astype(jnp.bfloat16)
        grad_tokens = tokens_sum.astype(jnp.bfloat16)
        return (ffn_output, grad_tokens, grad_up, grad_down, grad_up_bias.reshape(hidden))

    return on_device


def plain_program(
    tokens, up_codes, up_scales, up_bias, down_codes, down_scales, down_bias, cotangent
):
    w_up = dequantize(up_codes, up_scales)
    w_down = dequantize(down_codes, down_scales)
    cot_rows = lax.all_gather(cotangent, "hidden", axis=0, tiled=True)
    token_rows = lax.all_gather(tokens, "hidden", axis=0, tiled=True)
    bias_up = up_bias.astype(jnp.float32)

    def summed(share, axis):
        return lax.psum_scatter(
            share.astype(jnp.bfloat16), axis, scatter_dimension=0, tiled=True
        ).astype(jnp.float32)

    preact_share = summed(plain_product(token_rows, w_up), "mp") + bias_up
    act_share = gelu_value(preact_share).astype(jnp.bfloat16)
    act_rows = lax.all_gather(act_share, "mp", axis=0, tiled=True)
    grad_share = summed(product_transposed(cot_rows, w_down), "mp")
    grad_pre_share = (grad_share * gelu_slope(preact_share)).astype(jnp.bfloat16)
    grad_pre_rows = lax.all_gather(grad_pre_share, "mp", axis=0, tiled=True)
    output_sum = summed(plain_product(act_rows, w_down), "hidden")
    ffn_output = (output_sum + down_bias.astype(jnp.float32)).astype(jnp.bfloat16)
    grad_tokens = summed(product_transposed(grad_pre_rows, w_up), "hidden").astype(jnp.bfloat16)
    grad_up_bias = jnp.sum(grad_pre_rows, axis=0, dtype=jnp.float32)
    grad_down = transposed_product(act_rows, cot_rows).astype(jnp.bfloat16)
    grad_up = transposed_product(token_rows, grad_pre_rows).astype(jnp.bfloat16)
    return (ffn_output, grad_tokens, grad_up, grad_down, grad_up_bias)


def solution(mesh):
    mp_count, hidden_count = mesh.shape["mp"], mesh.shape["hidden"]

    def on_device(*arrays):
        hidden = arrays[1].shape[1]
        whole_blocks = hidden % (mp_count * LANES) == 0
        if whole_blocks and mp_count > 1 and hidden_count & (hidden_count - 1) == 0:
            return ring_program(mp_count, hidden_count)(*arrays)
        return plain_program(*arrays)

    in_specs = (
        P(("groups", "hidden"), "mp"),
        P("mp", "hidden"),
        P("mp", "hidden"),
        P("hidden"),
        P("hidden", "mp"),
        P("hidden", "mp"),
        P("mp"),
        P(("groups", "hidden"), "mp"),
    )
    out_specs = (
        P(("groups", "hidden"), "mp"),
        P(("groups", "hidden"), "mp"),
        P(("groups", "mp"), "hidden"),
        P(("groups", "hidden"), "mp"),
        P(("groups", "hidden")),
    )
    return jax.shard_map(
        on_device, mesh=mesh, in_specs=in_specs, out_specs=out_specs, check_vma=False
    )
```

```python
import functools

import jax
import jax.numpy as jnp
from jax import lax
from jax.experimental import pallas as pl
from jax.experimental.pallas import tpu as pltpu
from jax.sharding import PartitionSpec as P

root_two_pi = 0.7978845608028654
cubic_coef = 0.044715
LANES = 128
MIB = 1024 * 1024
SHARE_COST = 3
GRADIENT_COST = 3
SHARE_MIB = 4
GRADIENT_MIB = 12
DOWN_UNROLL = 3
GRADIENT_UNROLL = 2
KEEP_UP = (0, 3)
KEEP_DOWN = (0, 2, 3)


def gelu_value(argument):
    inner_arg = root_two_pi * (argument + cubic_coef * argument * argument * argument)
    return 0.5 * argument * (1.0 + jnp.tanh(inner_arg))


def gelu_slope(argument):
    inner_arg = root_two_pi * (argument + cubic_coef * argument * argument * argument)
    tangent = jnp.tanh(inner_arg)
    return 0.5 * (1.0 + tangent) + 0.5 * argument * (1.0 - tangent * tangent) * root_two_pi * (
        1.0 + 3.0 * cubic_coef * argument * argument
    )


def dequantize(weight_codes, block_scales):
    row_count, col_count = weight_codes.shape
    scale_rows, scale_cols = block_scales.shape
    blocks = weight_codes.astype(jnp.float32).reshape(
        scale_rows, row_count // scale_rows, scale_cols, col_count // scale_cols
    )
    scaled = blocks * block_scales[:, None, :, None]
    return scaled.reshape(row_count, col_count).astype(jnp.bfloat16)


def plain_product(left_side, right_side):
    return jnp.dot(left_side, right_side, preferred_element_type=jnp.float32)


def product_transposed(left_side, right_side):
    return lax.dot_general(
        left_side, right_side, (((1,), (1,)), ((), ())), preferred_element_type=jnp.float32
    )


def transposed_product(left_side, right_side):
    return lax.dot_general(
        left_side, right_side, (((0,), (0,)), ((), ())), preferred_element_type=jnp.float32
    )


def span(first, count):
    return pl.ds(pl.multiple_of(first, LANES), count)


def up_scaled(side, weights_ref, scales_ref, block, first, count):
    columns = span(first, count)
    scale_columns = span(block * weights_ref.shape[1] + first, count)
    for row in range(weights_ref.shape[0] // side):
        rows = slice(row * side, (row + 1) * side)
        weights_ref[rows, columns] = (
            weights_ref[rows, columns].astype(jnp.float32) * scales_ref[row : row + 1, scale_columns]
        ).astype(jnp.bfloat16)
    return weights_ref[:, columns]


def down_scaled(side, weights_ref, scales_ref, block, first, count):
    for row in range(count // side):
        rows = span(first + row * side, side)
        weights_ref[rows, :] = (
            weights_ref[rows, :].astype(jnp.float32)
            * scales_ref[block, pl.ds(first // side + row, 1), :]
        ).astype(jnp.bfloat16)
    return weights_ref[span(first, count), :]


def code_copy(up, piece, codes_ref, weights_ref, sems, block, index):
    block_width = weights_ref.shape[1 if up else 0]
    there = span(block * block_width + index * piece, piece)
    here = span(index * piece, piece)
    return pltpu.make_async_copy(
        codes_ref.at[:, there] if up else codes_ref.at[there, :],
        weights_ref.at[:, here] if up else weights_ref.at[here, :],
        sems.at[index],
    )


def each(count, body, unroll=1):
    def step(index, nothing):
        body(index)
        return nothing

    lax.fori_loop(0, count, step, None, unroll=unroll)


def share_kernel(side, up, piece, part_count, sum_in, turn, block_ref, *refs):
    refs = list(refs)
    block = block_ref[0]
    parts = [refs.pop(0) for _ in range(part_count)]
    rows_ref = None if part_count else refs.pop(0)
    codes_ref, scales_ref = refs.pop(0), refs.pop(0)
    sum_ref = refs.pop(0) if sum_in else None
    out_ref = refs.pop(0)
    if part_count:
        rows_ref = refs.pop(0)
    turned_ref = refs.pop(0) if turn else None
    weights_ref, sems = refs.pop(0), refs.pop(0)
    sum_held = refs.pop(0) if sum_in else None
    count = out_ref.shape[1] // piece

    def copy(index):
        return code_copy(up, piece, codes_ref, weights_ref, sems, block, index)

    if part_count:
        depth = parts[0].shape[0]
        own_copy = pltpu.make_async_copy(parts[0], rows_ref.at[:depth, :], sems.at[count])
        own_copy.start()
    if sum_in:
        sum_copy = pltpu.make_async_copy(sum_ref, sum_held, sems.at[count])
        sum_copy.start()
    each(count, lambda index: copy(index).start())
    if part_count:
        for index, part in enumerate(parts):
            if index == 0:
                continue
            rows_ref[index * depth : (index + 1) * depth, :] = part[...]
        own_copy.wait()
    if turn:
        turned_ref[...] = rows_ref[...].T
    if sum_in:
        sum_copy.wait()

    def work(index):
        copy(index).wait()
        columns = span(index * piece, piece)
        if up:
            weights = up_scaled(side, weights_ref, scales_ref, block, index * piece, piece)
            share = plain_product(rows_ref[...], weights)
        else:
            weights = down_scaled(side, weights_ref, scales_ref, block, index * piece, piece)
            share = product_transposed(rows_ref[...], weights)
        if sum_in:
            share = share.astype(jnp.bfloat16).astype(jnp.float32) + sum_held[:, columns].astype(
                jnp.float32
            )
        out_ref[:, columns] = share.astype(jnp.bfloat16)

    each(count, work, 1 if up else DOWN_UNROLL)


def activation_kernel(sum_ref, share_ref, bias_ref, act_ref, slope_ref):
    preact = (
        sum_ref[...].astype(jnp.float32)
        + share_ref[...].astype(jnp.float32)
        + bias_ref[...].astype(jnp.float32)
    )
    act_ref[...] = gelu_value(preact).astype(jnp.bfloat16)
    slope_ref[...] = gelu_slope(preact)


def product_kernel(act_ref, weights_ref, total_in, after_ref, kept_ref, sent_ref):
    total = (total_in[...] + product_transposed(weights_ref[...], act_ref[...])).T
    half = total.shape[0] // 2
    kept_ref[...] = total[:half, :]
    sent_ref[...] = total[half:, :].astype(jnp.bfloat16)


def gradient_kernel(side, up, piece, fresh, last, kept_weights, summed, block_ref, *refs):
    refs = list(refs)
    block = block_ref[0]
    block_act, rows_ref = refs.pop(0), refs.pop(0)
    weights_ref = refs.pop(0) if kept_weights and summed else None
    codes_ref, scales_ref = (None, None) if kept_weights else (refs.pop(0), refs.pop(0))
    if not fresh:
        total_in = refs.pop(0) if summed else None
        refs.pop(0)
        bias_in = refs.pop(0) if up else None
    refs.pop(0)
    if last and summed:
        kept_ref, sent_ref = refs.pop(0), refs.pop(0)
    elif summed:
        total_ref = refs.pop(0)
    grad_ref = refs.pop(0)
    bias_ref = refs.pop(0) if up else None
    if last and summed:
        total_ref = refs.pop(0)
    staged, out_sems = refs.pop(0), refs.pop(0)
    block_width = block_act.shape[1]
    count = block_width // piece

    def copy(index):
        return code_copy(up, piece, codes_ref, weights_ref, sems, block, index)

    def write(index):
        there = span(block * block_width + index * piece, piece)
        return pltpu.make_async_copy(
            staged.at[index], grad_ref.at[:, there] if up else grad_ref.at[there, :], out_sems.at[index]
        )

    if not kept_weights:
        weights_ref, sems = refs
        each(count, lambda index: copy(index).start())
    if up and not fresh:
        bias_ref[...] = bias_in[...]
    if summed:
        total_ref[...] = jnp.zeros_like(total_ref) if fresh else total_in[...]

    def work(index):
        columns = span(index * piece, piece)
        act = block_act[:, columns]
        if summed and not kept_weights:
            copy(index).wait()
            scaled = up_scaled if up else down_scaled
            scaled(side, weights_ref, scales_ref, block, index * piece, piece)
        if up:
            gradient = plain_product(rows_ref[...], act)
            bias_ref[0:1, span(block * block_width + index * piece, piece)] = jnp.sum(
                act.astype(jnp.float32), axis=0, keepdims=True
            )
        else:
            gradient = transposed_product(act, rows_ref[...])
        staged[index] = gradient.astype(jnp.bfloat16)
        if summed and up:
            total_ref[...] += product_transposed(weights_ref[:, columns], act)
        elif summed:
            total_ref[...] += plain_product(act, weights_ref[columns, :])
        write(index).start()

    each(count, work, GRADIENT_UNROLL)
    if last and summed:
        half = total_ref.shape[0] // 2
        kept_ref[...] = total_ref[:half, :]
        sent_ref[...] = total_ref[half:, :].astype(jnp.bfloat16)
    each(count, lambda index: write(index).wait())


def cost_of(scale, token_count, width, hidden_count, products, passes):
    return pl.CostEstimate(
        flops=int(scale * 2 * products * token_count * width * hidden_count),
        bytes_accessed=int(scale * 2 * passes * width * hidden_count),
        transcendentals=0,
    )


ANY_SPEC = pl.BlockSpec(memory_space=pl.ANY)
VMEM_SPEC = pl.BlockSpec(memory_space=pltpu.VMEM)
SMEM_SPEC = pl.BlockSpec(memory_space=pltpu.SMEM)


class Operands:
    def __init__(self, block):
        self.arrays, self.specs = [block], [SMEM_SPEC]

    def add(self, array, spec=VMEM_SPEC):
        self.arrays.append(array)
        self.specs.append(spec)


def call(name, kernel, operands, outs, scratch, cost, limit, aliases=None):
    return pl.pallas_call(
        kernel,
        in_specs=operands.specs,
        out_specs=[spec for _, spec in outs],
        scratch_shapes=scratch,
        out_shape=[shape for shape, _ in outs],
        input_output_aliases=aliases or {},
        cost_estimate=cost,
        name=name,
        compiler_params=pltpu.CompilerParams(vmem_limit_bytes=limit * MIB),
    )(*operands.arrays)


class Sizes:
    def __init__(self, rows, width, hidden, block_width, side):
        self.rows, self.width, self.hidden = rows, width, hidden
        self.block_width, self.side = block_width, side

    def piece(self, most):
        return next(
            size for size in (512, 256, 128) if size <= most and self.block_width % size == 0
        )

    def weights_shape(self, up):
        return (self.width, self.block_width) if up else (self.block_width, self.width)


def share_call(sizes, up, block, rows, codes, scales, sum_in, keep, turn=False):
    parts = rows if isinstance(rows, list) else []
    operands = Operands(block)
    for index, part in enumerate(parts or [rows]):
        if parts and index == 0:
            operands.add(pltpu.with_memory_space_constraint(part, pltpu.HBM), ANY_SPEC)
        else:
            operands.add(part)
    operands.add(pltpu.with_memory_space_constraint(codes, pltpu.HBM), ANY_SPEC)
    operands.add(scales)
    if sum_in is not None:
        operands.add(sum_in, ANY_SPEC)
    outs = [(pltpu.VMEM((sizes.rows, sizes.block_width), jnp.bfloat16), VMEM_SPEC)]
    if parts:
        outs.append((jax.ShapeDtypeStruct((sizes.rows, sizes.width), jnp.bfloat16), VMEM_SPEC))
    if turn:
        outs.append((jax.ShapeDtypeStruct((sizes.width, sizes.rows), jnp.bfloat16), VMEM_SPEC))
    weights = pltpu.VMEM(sizes.weights_shape(up), jnp.bfloat16)
    if keep:
        outs.append((weights, VMEM_SPEC))
    piece = sizes.piece(256 if up else 512)
    return call(
        "up_share" if up else "down_share",
        functools.partial(share_kernel, sizes.side, up, piece, len(parts), sum_in is not None, turn),
        operands,
        outs,
        ([] if keep else [weights])
        + [pltpu.SemaphoreType.DMA((sizes.block_width // piece + 1,))]
        + ([] if sum_in is None else [pltpu.VMEM((sizes.rows, sizes.block_width), jnp.bfloat16)]),
        cost_of(SHARE_COST, sizes.rows, sizes.width, sizes.block_width, 1, 1),
        SHARE_MIB if keep else SHARE_MIB + 7,
    )


def gradient_call(
    sizes, up, block, block_act, rows, weights, codes, scales, held, after, last, summed=True
):
    full_shape = (sizes.width, sizes.rows) if up else (sizes.rows, sizes.width)
    half_shape = (sizes.rows // 2, sizes.width)
    kept = weights is not None
    operands = Operands(block)
    operands.add(block_act)
    operands.add(rows)
    if kept and summed:
        operands.add(pltpu.with_memory_space_constraint(weights, pltpu.VMEM))
    elif not kept:
        operands.add(pltpu.with_memory_space_constraint(codes, pltpu.HBM), ANY_SPEC)
        operands.add(scales)
    fresh = held is None
    aliases = {}
    if not fresh:
        at = len(operands.arrays)
        if summed:
            aliases = {at + 1: 2 if last else 1}
            operands.add(held[0])
        else:
            aliases = {at: 0}
        operands.add(pltpu.with_memory_space_constraint(held[1], pltpu.HBM), ANY_SPEC)
        if up:
            operands.add(held[2])
    operands.add(after, ANY_SPEC)
    if not summed:
        outs = []
    elif last:
        outs = [
            (jax.ShapeDtypeStruct(half_shape, jnp.float32), VMEM_SPEC),
            (jax.ShapeDtypeStruct(half_shape, jnp.bfloat16), VMEM_SPEC),
        ]
    else:
        outs = [(jax.ShapeDtypeStruct(full_shape, jnp.float32), VMEM_SPEC)]
    outs.append((pltpu.HBM(codes.shape, jnp.bfloat16), ANY_SPEC))
    if up:
        outs.append((jax.ShapeDtypeStruct((1, sizes.hidden), jnp.float32), VMEM_SPEC))
    piece = sizes.piece(256)
    slot_shape = (sizes.width, piece) if up else (piece, sizes.width)
    slots = sizes.block_width // piece
    scratch = [pltpu.VMEM(full_shape, jnp.float32)] if last and summed else []
    scratch += [pltpu.VMEM((slots,) + slot_shape, jnp.bfloat16), pltpu.SemaphoreType.DMA((slots,))]
    if not kept:
        scratch += [
            pltpu.VMEM(sizes.weights_shape(up), jnp.bfloat16),
            pltpu.SemaphoreType.DMA((sizes.block_width // piece,)),
        ]
    return call(
        "up_gradient" if up else "down_gradient",
        functools.partial(gradient_kernel, sizes.side, up, piece, fresh, last, kept, summed),
        operands,
        outs,
        scratch,
        cost_of(GRADIENT_COST, sizes.rows, sizes.width, sizes.block_width, 2, 2 if summed else 1),
        GRADIENT_MIB if kept else GRADIENT_MIB + 7,
        aliases,
    )


def activation_call(sizes, sum_in, share, bias):
    block_shape = (sizes.rows, sizes.block_width)
    return pl.pallas_call(
        activation_kernel,
        in_specs=[VMEM_SPEC] * 3,
        out_specs=[VMEM_SPEC] * 2,
        out_shape=[
            jax.ShapeDtypeStruct(block_shape, jnp.bfloat16),
            jax.ShapeDtypeStruct(block_shape, jnp.float32),
        ],
        name="activation",
        compiler_params=pltpu.CompilerParams(vmem_limit_bytes=SHARE_MIB * MIB),
    )(sum_in, share, bias)


def product_call(sizes, block_act, weights, total_in, after):
    half_shape = (sizes.rows // 2, sizes.width)
    return pl.pallas_call(
        product_kernel,
        in_specs=[VMEM_SPEC] * 3 + [ANY_SPEC],
        out_specs=[VMEM_SPEC] * 2,
        out_shape=[
            jax.ShapeDtypeStruct(half_shape, jnp.float32),
            jax.ShapeDtypeStruct(half_shape, jnp.bfloat16),
        ],
        cost_estimate=cost_of(SHARE_COST, sizes.rows, sizes.width, sizes.block_width, 1, 1),
        name="last_product",
        compiler_params=pltpu.CompilerParams(vmem_limit_bytes=SHARE_MIB * MIB),
    )(block_act, pltpu.with_memory_space_constraint(weights, pltpu.VMEM), total_in, after)


def ring_program(mp_count, hidden_count):
    order = [0, *range(1, mp_count, 2), *reversed(range(2, mp_count, 2))]
    ring = [(order[i], order[(i + 1) % mp_count]) for i in range(mp_count)]
    bits = [1 << bit for bit in reversed(range(hidden_count.bit_length() - 1))]

    def partner_pairs(bit):
        return [(i, i ^ bit) for i in range(hidden_count)]

    def after(array, *earlier):
        return lax.optimization_barrier((array, *earlier))[0]

    def first_exchange(own_rows):
        return [own_rows, lax.ppermute(own_rows, "hidden", partner_pairs(bits[0]))]

    def later_exchanges(held, *earlier):
        held = [held[0], after(held[1], *earlier)] if earlier else held
        for bit in bits[1:]:
            held = held + [lax.ppermute(part, "hidden", partner_pairs(bit)) for part in held]
        return held

    def scattered_sum(kept, sent):
        for bit in reversed(bits):
            kept = kept + lax.ppermute(sent, "hidden", partner_pairs(bit)).astype(jnp.float32)
            half = kept.shape[0] // 2
            if bit != bits[0]:
                kept, sent = kept[:half], kept[half:].astype(jnp.bfloat16)
        return kept, sent

    def passed_on(block):
        return lax.ppermute(block, "mp", ring)

    def added(left, right):
        return left.astype(jnp.float32) + right.astype(jnp.float32)

    def on_device(
        tokens, up_codes, up_scales, up_bias, down_codes, down_scales, down_bias, cotangent
    ):
        width, hidden = up_codes.shape
        side = width // up_scales.shape[0]
        block_width = hidden // mp_count
        sizes = Sizes(tokens.shape[0] * hidden_count, width, hidden, block_width, side)
        index = lax.axis_index("mp").astype(jnp.int32)
        me = jnp.where(index % 2 == 1, (index + 1) // 2, (mp_count - index // 2) % mp_count)

        up_wide = jnp.repeat(up_scales, side, axis=1)
        down_wide = jnp.repeat(down_scales, side, axis=1).reshape(mp_count, -1, width)
        own_bias = lax.dynamic_slice(
            up_bias.reshape(1, hidden), (0, me * block_width), (1, block_width)
        )
        token_rows = first_exchange(tokens)
        cot_rows = first_exchange(after(cotangent, up_wide, down_wide, own_bias))
        token_rows = later_exchanges(token_rows, up_wide, down_wide, own_bias)

        def block_number(back):
            return ((me + 2 * mp_count - back) % mp_count).reshape(1)

        up_weights, down_weights = {}, {}

        def up_share(back, rows, sum_in, turn, *earlier):
            block = after(block_number(back), *earlier)
            made = share_call(
                sizes, True, block, rows, up_codes, up_wide, sum_in, back in KEEP_UP, turn
            )
            if back in KEEP_UP:
                up_weights[back] = made[-1]
            return made

        def down_share(back, rows, sum_in, *earlier):
            block = after(block_number(back), *earlier)
            made = share_call(
                sizes, False, block, rows, down_codes, down_wide, sum_in, back in KEEP_DOWN
            )
            if back in KEEP_DOWN:
                down_weights[back] = made[-1]
            return made

        up_part, token_rows, *made = up_share(1, token_rows, None, mp_count == 2)
        turned_tokens = made[0] if mp_count == 2 else None
        up_sum = passed_on(up_part)
        down_part, cot_rows, *_ = down_share(1, later_exchanges(cot_rows, up_part), None)
        down_sum = passed_on(down_part)
        for back in range(2, mp_count):
            last = back == mp_count - 1
            up_part, *made = up_share(back, token_rows, up_sum, last)
            up_sum = passed_on(up_part)
            if last:
                turned_tokens = made[0]
                own_part = up_share(0, token_rows, None, False, up_part)[0]
            down_part = down_share(back, cot_rows, down_sum, *([own_part] if last else []))[0]
            down_sum = passed_on(down_part)
        if mp_count == 2:
            own_part = up_share(0, token_rows, None, False, up_part)[0]
        act_block, slope = activation_call(sizes, up_sum, own_part, own_bias)
        down_part = down_share(0, cot_rows, None, act_block)[0]
        pre_block = (added(down_sum, down_part) * slope).astype(jnp.bfloat16)

        output_held = input_held = None
        for back in range(mp_count):
            last = back == mp_count - 1
            sent_act = act_block if back == 0 else after(act_block, output_held[0])
            next_act = None if last else passed_on(sent_act)
            sent_pre = pre_block if back == 0 else after(pre_block, input_held[0])
            next_pre = None if last else passed_on(sent_pre)
            output_held = gradient_call(
                sizes, False, block_number(back), act_block, cot_rows, down_weights.get(back),
                down_codes, down_wide, output_held,
                pre_block if back == 0 else input_held[0], last,
            )
            if last:
                output_sum, output_sent = scattered_sum(output_held[0], output_held[1])
                tokens_kept, tokens_sent = product_call(
                    sizes, pre_block, up_weights[back], input_held[0], output_held[1]
                )
                tokens_sum, tokens_sent = scattered_sum(tokens_kept, tokens_sent)
                ordering = after(tokens_sent, output_sent)
            else:
                ordering = output_held[0]
            input_held = gradient_call(
                sizes, True, block_number(back), pre_block, turned_tokens, up_weights.get(back),
                up_codes, up_wide, input_held, ordering, last, not last,
            )
            act_block, pre_block = next_act, next_pre
        grad_down = output_held[-1]
        grad_up, grad_up_bias = input_held
        ffn_output = (output_sum + down_bias.astype(jnp.float32)).astype(jnp.bfloat16)
        grad_tokens = tokens_sum.astype(jnp.bfloat16)
        return (ffn_output, grad_tokens, grad_up, grad_down, grad_up_bias.reshape(hidden))

    return on_device


def plain_program(
    tokens, up_codes, up_scales, up_bias, down_codes, down_scales, down_bias, cotangent
):
    w_up = dequantize(up_codes, up_scales)
    w_down = dequantize(down_codes, down_scales)
    cot_rows = lax.all_gather(cotangent, "hidden", axis=0, tiled=True)
    token_rows = lax.all_gather(tokens, "hidden", axis=0, tiled=True)
    bias_up = up_bias.astype(jnp.float32)

    def summed(share, axis):
        return lax.psum_scatter(
            share.astype(jnp.bfloat16), axis, scatter_dimension=0, tiled=True
        ).astype(jnp.float32)

    preact_share = summed(plain_product(token_rows, w_up), "mp") + bias_up
    act_share = gelu_value(preact_share).astype(jnp.bfloat16)
    act_rows = lax.all_gather(act_share, "mp", axis=0, tiled=True)
    grad_share = summed(product_transposed(cot_rows, w_down), "mp")
    grad_pre_share = (grad_share * gelu_slope(preact_share)).astype(jnp.bfloat16)
    grad_pre_rows = lax.all_gather(grad_pre_share, "mp", axis=0, tiled=True)
    output_sum = summed(plain_product(act_rows, w_down), "hidden")
    ffn_output = (output_sum + down_bias.astype(jnp.float32)).astype(jnp.bfloat16)
    grad_tokens = summed(product_transposed(grad_pre_rows, w_up), "hidden").astype(jnp.bfloat16)
    grad_up_bias = jnp.sum(grad_pre_rows, axis=0, dtype=jnp.float32)
    grad_down = transposed_product(act_rows, cot_rows).astype(jnp.bfloat16)
    grad_up = transposed_product(token_rows, grad_pre_rows).astype(jnp.bfloat16)
    return (ffn_output, grad_tokens, grad_up, grad_down, grad_up_bias)


def solution(mesh):
    mp_count, hidden_count = mesh.shape["mp"], mesh.shape["hidden"]

    def on_device(*arrays):
        hidden = arrays[1].shape[1]
        whole_blocks = hidden % (mp_count * LANES) == 0
        if whole_blocks and mp_count > 1 and hidden_count & (hidden_count - 1) == 0:
            return ring_program(mp_count, hidden_count)(*arrays)
        return plain_program(*arrays)

    in_specs = (
        P(("groups", "hidden"), "mp"),
        P("mp", "hidden"),
        P("mp", "hidden"),
        P("hidden"),
        P("hidden", "mp"),
        P("hidden", "mp"),
        P("mp"),
        P(("groups", "hidden"), "mp"),
    )
    out_specs = (
        P(("groups", "hidden"), "mp"),
        P(("groups", "hidden"), "mp"),
        P(("groups", "mp"), "hidden"),
        P(("groups", "hidden"), "mp"),
        P(("groups", "hidden")),
    )
    return jax.shard_map(
        on_device, mesh=mesh, in_specs=in_specs, out_specs=out_specs, check_vma=False
    )
```
